32 devices in a mesh: group: 2 (over y), state: 8 (over z, x), sample: 2 (over core).
Axes of the slice: x: 2, y: 2, z: 4, core: 2. Of those that a mesh axis runs over, the one named last changes fastest.
Arguments:
- energies: float32 [512, 65536], P(('group', 'state'), 'sample'), parts along dimension 0, may hold values from -300 to 8
- counts: int32 [512], P(('group', 'state')), parts along dimension 0, may hold values from 1 to 256
- labels: int32 [131072], P(('group', 'sample')), parts along dimension 0, may hold values from 0 to 255
- free_energy: float32 [512], P(('group', 'state')), parts along dimension 0, may hold values from -6 to 6
- directions: float32 [2, 512], P(None, ('group', 'state')), parts along dimension 1, may hold values from -6 to 6
Outputs:
- log_norm: float32 [131072], P(('group', 'sample')), parts along dimension 0
- anchor_logp: float32 [131072], P(('group', 'sample')), parts along dimension 0
- gradient: float32 [512], P(('group', 'state')), parts along dimension 0
- hessian_products: float32 [2, 512], P(None, ('group', 'state')), parts along dimension 1
The draws below stay inside these ranges and needn't reach their ends.
There are 2 independent parts, one for each index of `group`. The reference program is written for one: setup_inputs(seed, part) draws one part's arguments, and reference() takes and returns one part's arrays. A program takes and returns all parts, laid end to end along the dimension named above; each array names one. Nothing has to cross between parts.
All inputs are finite; a program needn't handle non-finite values.
Results may differ from the reference program's by a relative error of at most 0.0003.
Values sent between devices are 32-bit elements; how exact they have to be, the bound alone decides.
No kernel may reach another device: no remote copies, remote signals or barrier semaphores. Data moves between devices by JAX's collectives and lax.ppermute only.
A program may use at most 64 MiB of HBM per device.

```python
import math
import jax
import jax.numpy as jnp
from jax import lax

STATES = 256
SAMPLES = 65536


def draw_energies(key, part):
    key_noise = jax.random.fold_in(key, 0)
    ramp = jnp.arange(STATES, dtype=jnp.float32)[:, None] / STATES
    noise = jnp.clip(jax.random.normal(key_noise, (STATES, SAMPLES), jnp.float32), -6.0, 6.0)
    return noise - 1.1 * ramp


def with_ends(entries, own_key, low, high):
    longest = entries.shape.index(max(entries.shape))
    spots = []
    for shift in (0, 1):
        where = [jax.random.randint(jax.random.fold_in(own_key, axis), (), 0, length) for axis, length in enumerate(entries.shape)]
        where[longest] = (where[longest] + shift) % entries.shape[longest]
        spots.append(tuple(where))
    return entries.at[spots[0]].set(low).at[spots[1]].set(high)


def shard_levels(own_key, shape, shards, low, high):
    def one(dim, blocks):
        heights = jax.random.uniform(jax.random.fold_in(jax.random.fold_in(own_key, 6), dim), (blocks,), jnp.float32, low / len(shards), high / len(shards))
        return jnp.repeat(jnp.exp(heights), shape[dim] // blocks).reshape((-1,) + (1,) * (len(shape) - dim - 1))

    gain = one(*shards[0])
    for cut in shards[1:]:
        gain = gain * one(*cut)
    return gain


def scatter_about(key, extent, deviation, most, cuts=(), kind=jnp.bfloat16):
    entries = jax.random.normal(key, extent, jnp.float32) * deviation
    if len(cuts) > 0:
        entries = shard_levels(key, extent, cuts, -0.22, 0.18) * entries
    return jnp.clip(entries, min=-most, max=most).astype(kind)


def setup_inputs(seed: int = 0, part: int = 0) -> dict:
    keys = jax.random.split(jax.random.key(seed), 6)
    part_keys = jax.random.split(jax.random.fold_in(keys[5], part), 6)
    return {
        "energies": draw_energies(jax.random.fold_in(jax.random.fold_in(keys[5], part), 71), part),
        "counts": with_ends(jax.random.randint(part_keys[1], (STATES,), 1, 257), jax.random.fold_in(part_keys[1], 1), 1, 256).astype(jnp.int32),
        "labels": with_ends(jax.random.randint(part_keys[2], (SAMPLES,), 0, STATES), jax.random.fold_in(part_keys[2], 1), 0, STATES - 1).astype(jnp.int32),
        "free_energy": scatter_about(part_keys[3], (STATES,), 1.0, 6.0, ((0, 8),), jnp.float32),
        "directions": scatter_about(part_keys[4], (2, STATES), 1.0, 6.0, ((1, 8),), jnp.float32),
    }


def reference(energies, counts, labels, free_energy, directions):
    block = math.gcd(SAMPLES, 4096)
    steps_count = SAMPLES // block
    base = jnp.log(counts.astype(jnp.float32)) + free_energy
    state_ids = jnp.arange(STATES, dtype=jnp.int32)

    def visit(carry, number):
        start = (number * block).astype(jnp.int32)
        energy_block = lax.dynamic_slice_in_dim(energies, start, block, 1)
        label_block = lax.dynamic_slice_in_dim(labels, start, block, 0)
        shifted = base[:, None] - energy_block
        peak = jnp.max(shifted, axis=0)
        norm_block = peak + jnp.log(jnp.sum(jnp.exp(shifted - peak[None, :]), axis=0))
        weights = jnp.exp(shifted - norm_block[None, :])
        mixed = jnp.dot(directions, weights, precision=lax.Precision.HIGHEST)
        matches = state_ids[:, None] == label_block[None, :]
        anchor = jnp.sum(jnp.where(matches, shifted, 0.0), axis=0) - norm_block
        occupancy = jnp.sum(weights, axis=1)
        tally = jnp.sum(matches.astype(jnp.float32), axis=1)
        curvature = directions * occupancy[None, :] - jnp.einsum("jn,kn->jk", mixed, weights, precision=lax.Precision.HIGHEST)
        new_carry = (carry[0] + (occupancy - tally), carry[1] + curvature)
        return new_carry, (norm_block, anchor)

    init = (jnp.zeros((STATES,), jnp.float32), jnp.zeros((2, STATES), jnp.float32))
    totals, outputs = lax.scan(visit, init, jnp.arange(steps_count, dtype=jnp.int32))
    scale = STATES / SAMPLES
    log_norm = outputs[0].reshape(SAMPLES)
    anchor_logp = outputs[1].reshape(SAMPLES)
    return log_norm, anchor_logp, scale * totals[0], scale * totals[1]
```

```python
import functools
import math

import jax
import jax.numpy as jnp
from jax import lax
from jax.experimental import pallas as pl
from jax.experimental.pallas import tpu as pltpu
from jax.sharding import PartitionSpec as P

LANES = 128
ROWS = 8
TILE = LANES * ROWS


def plan(level, shift):
    if level == 0:
        return [0] * ROWS, 1
    half = ROWS >> level
    first, count = plan(level - 1, shift)
    second, _ = plan(level - 1, shift - half)
    owner = []
    for row in range(ROWS):
        keep = ((row - shift) // half) % 2 == 1
        owner.append(first[row] if keep else second[row] + count)
    return owner, 2 * count


PLACE, _ = plan(3, 0)


def fold(leaf, combine, rows, level=3, shift=0, first=0):
    if level == 0:
        return leaf(PLACE.index(first))
    half = ROWS >> level
    count = 1 << (level - 1)
    a = fold(leaf, combine, rows, level - 1, shift, first)
    b = fold(leaf, combine, rows, level - 1, shift - half, first + count)
    keep = (((rows - shift + 2 * ROWS) // half) % 2) == 1
    out = []
    for one, two, how in zip(a, b, combine, strict=True):
        mine = jnp.where(keep, one, two)
        other = jnp.where(keep, two, one)
        out.append(how(mine, pltpu.roll(other, half, 0)))
    return tuple(out)


def column(row, states):
    spread = jnp.broadcast_to(row, (states, states))
    eye = lax.broadcasted_iota(jnp.int32, (states, states), 0) == lax.broadcasted_iota(jnp.int32, (states, states), 1)
    picked = jnp.sum(jnp.where(eye, spread, 0.0), axis=1, keepdims=True)
    return jnp.broadcast_to(picked, (states, LANES))


def bases(counts_ref, free_ref, states):
    return column(jnp.log(counts_ref[...].astype(jnp.float32)) + free_ref[...], states)


def over_tiles(x, how):
    parts = [x[i * ROWS : (i + 1) * ROWS] for i in range(x.shape[0] // ROWS)]
    return functools.reduce(how, parts)


def local_body(spots_ref, counts_ref, free_ref, dirs_ref, labels_ref, energies_ref, *refs):
    *out_refs, tally_ref, base_s, dir_s = refs
    states = energies_ref.shape[0]
    steps = energies_ref.shape[1] // TILE
    number = pl.program_id(0)

    @pl.when(number == 0)
    def _():
        base_s[...] = bases(counts_ref, free_ref, states)
        dir_s[0] = column(dirs_ref[0:1, :], states)
        dir_s[1] = column(dirs_ref[1:2, :], states)
        tally_ref[...] = jnp.zeros_like(tally_ref)

    rows = lax.broadcasted_iota(jnp.int32, (ROWS, LANES), 0)
    ids = lax.broadcasted_iota(jnp.int32, (states, LANES), 0)
    first_state = spots_ref[4]

    def step(out_ref, j, tally):
        at = pl.multiple_of(j * ROWS, ROWS)
        labels = labels_ref[pl.ds(at, ROWS), :] - first_state
        base = base_s[...]

        def shifted(g):
            cols = pl.ds(pl.multiple_of(j * TILE + g * LANES, LANES), LANES)
            return base - energies_ref[:, cols]

        (peak,) = fold(lambda g: (over_tiles(shifted(g), jnp.maximum),), (jnp.maximum,), rows)
        matched = []

        def leaf(g):
            s = shifted(g)
            e = jnp.exp(s - jnp.broadcast_to(peak[g : g + 1, :], (states, LANES)))
            match = ids == jnp.broadcast_to(labels[g : g + 1, :], (states, LANES))
            matched.append(match.astype(jnp.float32))
            return (
                over_tiles(e, jnp.add),
                over_tiles(e * dir_s[0], jnp.add),
                over_tiles(e * dir_s[1], jnp.add),
                over_tiles(jnp.where(match, s, 0.0), jnp.add),
            )

        total, mix0, mix1, anchor = fold(leaf, (jnp.add,) * 4, rows)
        inverse = 1.0 / total
        out_ref[0, pl.ds(at, ROWS), :] = peak + jnp.log(total)
        out_ref[1, pl.ds(at, ROWS), :] = mix0 * inverse
        out_ref[2, pl.ds(at, ROWS), :] = mix1 * inverse
        out_ref[3, pl.ds(at, ROWS), :] = anchor
        return tally + functools.reduce(jnp.add, matched)

    for k, out_ref in enumerate(out_refs):

        @pl.when(number == k)
        def _():
            tally_ref[...] += lax.fori_loop(
                0, steps, functools.partial(step, out_ref), jnp.zeros((states, LANES), jnp.float32)
            )


def local_sums(spots, which, counts, free_energy, directions, labels, energies):
    states, samples = energies.shape
    width = samples // 4
    n = len(which)
    lo = which[0]
    whole = pl.BlockSpec(memory_space=pltpu.VMEM)
    part = jax.ShapeDtypeStruct((4, width // LANES, LANES), jnp.float32)
    fixed = pl.BlockSpec((4, width // LANES, LANES), lambda i, s: (0, 0, 0))
    return pl.pallas_call(
        local_body,
        grid_spec=pltpu.PrefetchScalarGridSpec(
            num_scalar_prefetch=1,
            grid=(n,),
            in_specs=[
                pl.BlockSpec((1, states), lambda i, s: (0, 0)),
                pl.BlockSpec((1, states), lambda i, s: (0, 0)),
                pl.BlockSpec((2, states), lambda i, s: (0, 0)),
                pl.BlockSpec((width // LANES, LANES), lambda i, s: (s[lo + i], 0)),
                pl.BlockSpec((states, width), lambda i, s: (0, s[lo + i])),
            ],
            out_specs=[fixed] * n + [pl.BlockSpec((states, LANES), lambda i, s: (0, 0))],
            scratch_shapes=[pltpu.VMEM((states, LANES), jnp.float32), pltpu.VMEM((2, states, LANES), jnp.float32)],
        ),
        out_shape=[part] * n + [jax.ShapeDtypeStruct((states, LANES), jnp.float32)],
        compiler_params=pltpu.CompilerParams(vmem_limit_bytes=24 * 1024 * 1024),
        cost_estimate=pl.CostEstimate(
            flops=20 * n * states * width, bytes_accessed=4 * n * states * width, transcendentals=n * states * width
        ),
        name="local_sums",
    )(
        spots,
        counts.reshape(1, states),
        free_energy.reshape(1, states),
        directions,
        labels.reshape(samples // LANES, LANES),
        energies,
    )


def curve_body(spots_ref, counts_ref, free_ref, dirs_ref, energies_ref, *refs):
    n = len(refs) - 5
    part_refs = refs[:n]
    norm_ref, anchor_ref, sums_ref, base_s, acc_s = refs[n:]
    states = energies_ref.shape[0]
    steps = energies_ref.shape[1] // TILE
    number = pl.program_id(0)

    @pl.when(number == 0)
    def _():
        base_s[...] = bases(counts_ref, free_ref, states)
        acc_s[...] = jnp.zeros_like(acc_s)

    def step(part_ref, j, carry):
        occupancy, mix0, mix1 = carry
        at = pl.multiple_of(j * ROWS, ROWS)
        norm = part_ref[0, pl.ds(at, ROWS), :]
        norm_ref[pl.ds(at, ROWS), :] = norm
        anchor_ref[pl.ds(at, ROWS), :] = part_ref[3, pl.ds(at, ROWS), :] - norm
        first = part_ref[1, pl.ds(at, ROWS), :]
        second = part_ref[2, pl.ds(at, ROWS), :]
        base = base_s[...]
        for g in range(ROWS):
            cols = pl.ds(pl.multiple_of(j * TILE + g * LANES, LANES), LANES)
            spread = lambda x: jnp.broadcast_to(x[g : g + 1, :], (states, LANES))
            w = jnp.exp((base - energies_ref[:, cols]) - spread(norm))
            occupancy += w
            mix0 += w * spread(first)
            mix1 += w * spread(second)
        return occupancy, mix0, mix1

    for k, part_ref in enumerate(part_refs):

        @pl.when(number == k)
        def _():
            zero = jnp.zeros((states, LANES), jnp.float32)
            occupancy, mix0, mix1 = lax.fori_loop(0, steps, functools.partial(step, part_ref), (zero, zero, zero))
            acc_s[0] += occupancy
            acc_s[1] += mix0
            acc_s[2] += mix1

    @pl.when(number == n - 1)
    def _():
        sums_ref[...] = acc_s[...]


def curve_sums(spots, which, parts, counts, free_energy, directions, energies, outs):
    states, samples = energies.shape
    width = samples // 4
    n = len(which)
    lo = which[0]
    body = curve_body
    whole = pl.BlockSpec((4, width // LANES, LANES), lambda i, s: (0, 0, 0))
    quarter = pl.BlockSpec((width // LANES, LANES), lambda i, s: (s[lo + i], 0))
    in_specs = [
        pl.BlockSpec((1, states), lambda i, s: (0, 0)),
        pl.BlockSpec((1, states), lambda i, s: (0, 0)),
        pl.BlockSpec((2, states), lambda i, s: (0, 0)),
        pl.BlockSpec((states, width), lambda i, s: (0, s[lo + i])),
    ] + [whole] * n
    args = [
        spots,
        counts.reshape(1, states),
        free_energy.reshape(1, states),
        directions,
        energies,
        *parts,
    ]
    aliases = {}
    if outs is not None:
        in_specs = in_specs + [pl.BlockSpec(memory_space=pl.ANY)] * 2
        aliases = {len(args): 0, len(args) + 1: 1}
        args += list(outs)

        def body(*refs):
            head = 5 + n
            return curve_body(*refs[:head], *refs[head + 2 :])

    long = jax.ShapeDtypeStruct((samples // LANES, LANES), jnp.float32)
    return pl.pallas_call(
        body,
        grid_spec=pltpu.PrefetchScalarGridSpec(
            num_scalar_prefetch=1,
            grid=(n,),
            in_specs=in_specs,
            out_specs=[quarter, quarter, pl.BlockSpec((3, states, LANES), lambda i, s: (0, 0, 0))],
            scratch_shapes=[pltpu.VMEM((states, LANES), jnp.float32), pltpu.VMEM((3, states, LANES), jnp.float32)],
        ),
        out_shape=[long, long, jax.ShapeDtypeStruct((3, states, LANES), jnp.float32)],
        input_output_aliases=aliases,
        compiler_params=pltpu.CompilerParams(vmem_limit_bytes=24 * 1024 * 1024),
        cost_estimate=pl.CostEstimate(
            flops=9 * n * states * width, bytes_accessed=4 * n * states * width, transcendentals=n * states * width
        ),
        name="curve_sums",
    )(*args)


def merge(parts):
    norms = [part[0:1] for part in parts]
    peak = functools.reduce(jnp.maximum, norms)
    scales = [jnp.exp(norm - peak) for norm in norms]
    total = functools.reduce(jnp.add, scales)
    mixed = functools.reduce(jnp.add, [s * part for s, part in zip(scales, parts, strict=True)]) / total
    anchor = functools.reduce(jnp.add, parts)
    kind = lax.broadcasted_iota(jnp.int32, parts[0].shape, 0)
    return jnp.where(kind == 0, peak + jnp.log(total), jnp.where(kind == 3, anchor, mixed))


def swap(x, width, cores, flips):
    pairs = []
    for place in range(width):
        for core in range(cores):
            pairs.append((place * cores + core, (place ^ flips[core]) * cores + core))
    return lax.ppermute(x, ("state", "sample"), pairs)


def local(energies, counts, labels, free_energy, directions):
    states, samples = energies.shape
    width, cores = lax.axis_size("state"), lax.axis_size("sample")
    place, core = lax.axis_index("state"), lax.axis_index("sample")
    rounds = [[3] * cores, [1 + c % 2 for c in range(cores)], [2 - c % 2 for c in range(cores)]]
    mine = place % 4
    turn = core % 2
    spots = jnp.stack([mine ^ 3, mine ^ (1 + turn), mine ^ (2 - turn), mine, place * states]).astype(jnp.int32)

    *sent, tally_a = local_sums(spots, (0, 1, 2), counts, free_energy, directions, labels, energies)
    got = [swap(x, width, cores, flips) for x, flips in zip(sent, rounds, strict=True)]
    own, tally_b = local_sums(spots, (3,), counts, free_energy, directions, labels, energies)
    part = merge([own, *got])
    for far in range(2, int(math.log2(width))):
        part = merge([part, swap(part, width, cores, [1 << far] * cores)])
    others = [swap(part, width, cores, flips) for flips in rounds]
    *outs, sums_a = curve_sums(spots, (3,), [part], counts, free_energy, directions, energies, None)
    log_norm, anchor_logp, sums_b = curve_sums(
        spots, (0, 1, 2), others, counts, free_energy, directions, energies, outs
    )
    sums = jnp.sum(sums_a + sums_b, axis=2)
    tally = jnp.sum(tally_a + tally_b, axis=1)
    summed = jnp.concatenate([(sums[0] - tally)[None, :], directions * sums[0][None, :] - sums[1:3]], axis=0)
    summed = lax.psum(summed, "sample")
    scale = states * width / (samples * cores)
    return (log_norm.reshape(samples), anchor_logp.reshape(samples), scale * summed[0], scale * summed[1:3])


def solution(mesh):
    return jax.shard_map(
        local,
        mesh=mesh,
        in_specs=(
            P(("group", "state"), "sample"),
            P(("group", "state")),
            P(("group", "sample")),
            P(("group", "state")),
            P(None, ("group", "state")),
        ),
        out_specs=(
            P(("group", "sample")),
            P(("group", "sample")),
            P(("group", "state")),
            P(None, ("group", "state")),
        ),
        check_vma=False,
    )
```

```python
import functools
import math

import jax
import jax.numpy as jnp
from jax import lax
from jax.experimental import pallas as pl
from jax.experimental.pallas import tpu as pltpu
from jax.sharding import PartitionSpec as P

LANES = 128
ROWS = 8
TILE = LANES * ROWS


def plan(level, shift):
    if level == 0:
        return [0] * ROWS, 1
    half = ROWS >> level
    first, count = plan(level - 1, shift)
    second, _ = plan(level - 1, shift - half)
    owner = []
    for row in range(ROWS):
        keep = ((row - shift) // half) % 2 == 1
        owner.append(first[row] if keep else second[row] + count)
    return owner, 2 * count


PLACE, _ = plan(3, 0)


def fold(leaf, combine, rows, level=3, shift=0, first=0):
    if level == 0:
        return leaf(PLACE.index(first))
    half = ROWS >> level
    count = 1 << (level - 1)
    a = fold(leaf, combine, rows, level - 1, shift, first)
    b = fold(leaf, combine, rows, level - 1, shift - half, first + count)
    keep = (((rows - shift + 2 * ROWS) // half) % 2) == 1
    out = []
    for one, two, how in zip(a, b, combine, strict=True):
        mine = jnp.where(keep, one, two)
        other = jnp.where(keep, two, one)
        out.append(how(mine, pltpu.roll(other, half, 0)))
    return tuple(out)


def column(row, states):
    spread = jnp.broadcast_to(row, (states, states))
    eye = lax.broadcasted_iota(jnp.int32, (states, states), 0) == lax.broadcasted_iota(jnp.int32, (states, states), 1)
    picked = jnp.sum(jnp.where(eye, spread, 0.0), axis=1, keepdims=True)
    return jnp.broadcast_to(picked, (states, LANES))


def bases(counts_ref, free_ref, states):
    return column(jnp.log(counts_ref[...].astype(jnp.float32)) + free_ref[...], states)


def spot(flips):
    core = lax.axis_index("sample")
    flip = functools.reduce(lambda rest, c: jnp.where(core == c, flips[c], rest), range(1, len(flips)), flips[0])
    return jnp.bitwise_xor(jnp.bitwise_and(lax.axis_index("state"), 3), flip)


def over_tiles(x, how):
    parts = [x[i * ROWS : (i + 1) * ROWS] for i in range(x.shape[0] // ROWS)]
    return functools.reduce(how, parts)


def spread(x, g, states):
    return jnp.broadcast_to(x[g : g + 1, :], (states, LANES))


def sums_of(out_ref, energies_ref, offset, labels_ref, label_row, base, dirs, first_state, steps):
    states = energies_ref.shape[0]
    rows = lax.broadcasted_iota(jnp.int32, (ROWS, LANES), 0)
    ids = lax.broadcasted_iota(jnp.int32, (states, LANES), 0)

    def step(j, carry):
        at = pl.multiple_of(j * ROWS, ROWS)
        labels = labels_ref[pl.ds(pl.multiple_of(label_row + j * ROWS, ROWS), ROWS), :] - first_state

        def shifted(g):
            cols = pl.ds(pl.multiple_of(offset + j * TILE + g * LANES, LANES), LANES)
            return base[...] - energies_ref[:, cols]

        (peak,) = fold(lambda g: (over_tiles(shifted(g), jnp.maximum),), (jnp.maximum,), rows)

        def leaf(g):
            s = shifted(g)
            e = jnp.exp(s - spread(peak, g, states))
            return (
                over_tiles(e, jnp.add),
                over_tiles(e * dirs[0], jnp.add),
                over_tiles(e * dirs[1], jnp.add),
                over_tiles(jnp.where(ids == spread(labels, g, states), s, 0.0), jnp.add),
            )

        total, mix0, mix1, anchor = fold(leaf, (jnp.add,) * 4, rows)
        inverse = 1.0 / total
        out_ref[0, pl.ds(at, ROWS), :] = peak + jnp.log(total)
        out_ref[1, pl.ds(at, ROWS), :] = mix0 * inverse
        out_ref[2, pl.ds(at, ROWS), :] = mix1 * inverse
        out_ref[3, pl.ds(at, ROWS), :] = anchor
        return carry

    lax.fori_loop(0, steps, step, 0)


def first_body(flips, counts_hbm, free_hbm, dirs_hbm, labels_hbm, energies_hbm, out_ref, base_out, dirs_out, *scratch):
    counts_s, free_s, dirs_s, labels_s, energies_s, sems = scratch
    states, samples = energies_hbm.shape
    width = samples // 4
    chunks = energies_s.shape[0]
    chunk = width // chunks
    quarter = spot(flips)
    rows = width // LANES
    small = [
        pltpu.make_async_copy(counts_hbm, counts_s, sems.at[0]),
        pltpu.make_async_copy(free_hbm, free_s, sems.at[1]),
        pltpu.make_async_copy(dirs_hbm, dirs_s, sems.at[2]),
        pltpu.make_async_copy(labels_hbm.at[pl.ds(pl.multiple_of(quarter * rows, rows), rows), :], labels_s, sems.at[3]),
    ]
    large = [
        pltpu.make_async_copy(
            energies_hbm.at[:, pl.ds(pl.multiple_of(quarter * width + c * chunk, chunk), chunk)],
            energies_s.at[c],
            sems.at[4 + c],
        )
        for c in range(chunks)
    ]
    for copy in small + large:
        copy.start()
    for copy in small:
        copy.wait()
    base_out[...] = bases(counts_s, free_s, states)
    dirs_out[0] = column(dirs_s[0:1, :], states)
    dirs_out[1] = column(dirs_s[1:2, :], states)
    first_state = lax.axis_index("state") * states
    for c, copy in enumerate(large):
        copy.wait()
        part = out_ref.at[:, pl.ds(c * (rows // chunks), rows // chunks), :]
        sums_of(
            part, energies_s.at[c], 0, labels_s, c * (rows // chunks), base_out, dirs_out, first_state, chunk // TILE
        )


def later_body(flips, base_ref, dirs_ref, labels_ref, energies_ref, out_ref):
    states, samples = energies_ref.shape
    width = samples // 4
    quarter = spot(flips)
    first_state = lax.axis_index("state") * states
    offset, row = quarter * width, quarter * (width // LANES)
    sums_of(out_ref, energies_ref, offset, labels_ref, row, base_ref, dirs_ref, first_state, width // TILE)


def tally_body(labels_ref, tally_ref):
    states = tally_ref.shape[0]
    first_state = lax.axis_index("state") * states
    ids = lax.broadcasted_iota(jnp.int32, (states, LANES), 0)

    def step(j, tally):
        labels = labels_ref[pl.ds(pl.multiple_of(j * ROWS, ROWS), ROWS), :] - first_state
        for g in range(ROWS):
            tally += jnp.where(ids == spread(labels, g, states), 1.0, 0.0)
        return tally

    tally_ref[...] = lax.fori_loop(0, labels_ref.shape[0] // ROWS, step, jnp.zeros((states, LANES), jnp.float32))


def weigh(part_ref, energies_ref, quarter, base_ref):
    states, samples = energies_ref.shape
    width = samples // 4

    def step(j, carry):
        occupancy, mix0, mix1 = carry
        at = pl.ds(pl.multiple_of(j * ROWS, ROWS), ROWS)
        norm, first, second = part_ref[0, at, :], part_ref[1, at, :], part_ref[2, at, :]
        for g in range(ROWS):
            cols = pl.ds(pl.multiple_of(quarter * width + j * TILE + g * LANES, LANES), LANES)
            w = jnp.exp((base_ref[...] - energies_ref[:, cols]) - spread(norm, g, states))
            occupancy += w
            mix0 += w * spread(first, g, states)
            mix1 += w * spread(second, g, states)
        return occupancy, mix0, mix1

    zero = jnp.zeros((states, LANES), jnp.float32)
    return lax.fori_loop(0, width // TILE, step, (zero, zero, zero))


def weigh_body(flips, *refs):
    n = len(flips)
    part_refs = refs[:n]
    base_ref, energies_ref, sums_ref = refs[n:]
    for k in range(n):
        for i, x in enumerate(weigh(part_refs[k], energies_ref, spot(flips[k]), base_ref)):
            if k == 0:
                sums_ref[i] = x
            else:
                sums_ref[i] += x


def last_body(flips, *refs):
    part_refs = refs[:4]
    base_ref, dirs_ref, tally_ref, sums_ref, energies_ref, norm_hbm, anchor_hbm, out_ref, sems = refs[4:]
    states, samples = energies_ref.shape
    rows = samples // 4 // LANES
    copies = []
    for k, part_ref in enumerate(part_refs):
        at = pl.ds(pl.multiple_of(spot(flips[k]) * rows, rows), rows)
        copies.append(pltpu.make_async_copy(part_ref.at[0], norm_hbm.at[at, :], sems.at[2 * k]))
        copies.append(pltpu.make_async_copy(part_ref.at[3], anchor_hbm.at[at, :], sems.at[2 * k + 1]))
    for copy in copies:
        copy.start()
    sums = weigh(part_refs[3], energies_ref, spot(flips[3]), base_ref)
    eye = lax.broadcasted_iota(jnp.int32, (states, states), 0) == lax.broadcasted_iota(jnp.int32, (states, states), 1)

    def row(x):
        total = jnp.broadcast_to(jnp.sum(x, axis=1, keepdims=True), (states, states))
        return jnp.sum(jnp.where(eye, total, 0.0), axis=0, keepdims=True)

    occupancy = sums[0] + sums_ref[0]
    out_ref[0:1, :] = row(occupancy - tally_ref[...])
    for j in range(2):
        out_ref[j + 1 : j + 2, :] = row(dirs_ref[j] * occupancy - (sums[j + 1] + sums_ref[j + 1]))
    for copy in copies:
        copy.wait()


def total_body(scale, mine_ref, other_ref, gradient_ref, products_ref):
    total = scale * (mine_ref[...] + other_ref[...])
    gradient_ref[...] = total[0:1]
    products_ref[...] = total[1:3]


VMEM = pl.BlockSpec(memory_space=pltpu.VMEM)
HBM = pl.BlockSpec(memory_space=pltpu.HBM)
LIMIT = 16 * 1024 * 1024


def f32(*shape):
    return jax.ShapeDtypeStruct(shape, jnp.float32)


def kernel(body, in_specs, out_specs, out_shape, name, work, scratch=()):
    return pl.pallas_call(
        body,
        in_specs=in_specs,
        out_specs=out_specs,
        out_shape=out_shape,
        scratch_shapes=list(scratch),
        compiler_params=pltpu.CompilerParams(vmem_limit_bytes=LIMIT),
        cost_estimate=pl.CostEstimate(flops=16 * work, bytes_accessed=4 * work, transcendentals=work),
        name=name,
    )


def merge(parts, last):
    norms = [part[0:1] for part in parts]
    peak = functools.reduce(jnp.maximum, norms)
    scales = [jnp.exp(norm - peak) for norm in norms]
    total = functools.reduce(jnp.add, scales)
    mixed = functools.reduce(jnp.add, [s * part for s, part in zip(scales, parts, strict=True)]) / total
    anchor = functools.reduce(jnp.add, parts)
    norm = peak + jnp.log(total)
    kind = lax.broadcasted_iota(jnp.int32, parts[0].shape, 0)
    return jnp.where(kind == 0, norm, jnp.where(kind == 3, anchor - norm if last else anchor, mixed))


def swap(x, width, cores, flips):
    pairs = []
    for place in range(width):
        for core in range(cores):
            pairs.append((place * cores + core, (place ^ flips[core]) * cores + core))
    return lax.ppermute(x, ("state", "sample"), pairs)


def local(energies, counts, labels, free_energy, directions):
    states, samples = energies.shape
    width, cores = lax.axis_size("state"), lax.axis_size("sample")
    rounds = [(3,) * cores, tuple(1 + c % 2 for c in range(cores)), tuple(2 - c % 2 for c in range(cores))]
    stay = (0,) * cores
    rows = samples // 4 // LANES
    work = states * samples // 4
    labels = labels.reshape(samples // LANES, LANES)
    part = f32(4, rows, LANES)
    chunks = 2 if samples % (8 * TILE) == 0 else 1

    first, base, dirs = kernel(
        functools.partial(first_body, rounds[0]),
        [HBM] * 5,
        [VMEM] * 3,
        [part, f32(states, LANES), f32(2, states, LANES)],
        "first_sums",
        work,
        [
            pltpu.VMEM((1, states), jnp.int32),
            pltpu.VMEM((1, states), jnp.float32),
            pltpu.VMEM((2, states), jnp.float32),
            pltpu.VMEM((rows, LANES), jnp.int32),
            pltpu.VMEM((chunks, states, samples // 4 // chunks), jnp.float32),
            pltpu.SemaphoreType.DMA((4 + chunks,)),
        ],
    )(
        *(
            pltpu.with_memory_space_constraint(x, pltpu.HBM)
            for x in (counts.reshape(1, states), free_energy.reshape(1, states), directions, labels, energies)
        )
    )

    def later(flips, name):
        return kernel(functools.partial(later_body, flips), [VMEM] * 4, VMEM, part, name, work)(
            base, dirs, labels, energies
        )

    sent = [first, later(rounds[1], "second_sums"), later(rounds[2], "third_sums")]
    got = [swap(x, width, cores, flips) for x, flips in zip(sent, rounds, strict=True)]
    own = later(stay, "own_sums")
    tally = kernel(tally_body, [VMEM], VMEM, f32(states, LANES), "tally", work)(labels)
    far = range(2, int(math.log2(width)))
    union = merge([own, *got], not far)
    for bit in far:
        union = merge([union, swap(union, width, cores, (1 << bit,) * cores)], bit == far[-1])
    others = [swap(union, width, cores, flips) for flips in rounds]
    sums = kernel(
        functools.partial(weigh_body, (stay, rounds[0], rounds[1])),
        [VMEM] * 5,
        VMEM,
        f32(3, states, LANES),
        "weigh",
        3 * work,
    )(union, others[0], others[1], base, energies)
    long = f32(samples // LANES, LANES)
    log_norm, anchor_logp, mine = kernel(
        functools.partial(last_body, (stay, *rounds)),
        [VMEM] * 9,
        [HBM, HBM, VMEM],
        [long, long, f32(3, states)],
        "last_sums",
        work,
        [pltpu.SemaphoreType.DMA((8,))],
    )(union, *others, base, dirs, tally, sums, energies)
    other = lax.ppermute(mine, "sample", [(c, cores - 1 - c) for c in range(cores)])
    gradient, products = kernel(
        functools.partial(total_body, states * width / (samples * cores)),
        [VMEM] * 2,
        [VMEM] * 2,
        [f32(1, states), f32(2, states)],
        "totals",
        1024,
    )(mine, other)
    return log_norm.reshape(samples), anchor_logp.reshape(samples), gradient.reshape(states), products


def solution(mesh):
    return jax.shard_map(
        local,
        mesh=mesh,
        in_specs=(
            P(("group", "state"), "sample"),
            P(("group", "state")),
            P(("group", "sample")),
            P(("group", "state")),
            P(None, ("group", "state")),
        ),
        out_specs=(
            P(("group", "sample")),
            P(("group", "sample")),
            P(("group", "state")),
            P(None, ("group", "state")),
        ),
        check_vma=False,
    )
```

```python
import functools
import math

import jax
import jax.numpy as jnp
from jax import lax
from jax.experimental import pallas as pl
from jax.experimental.pallas import tpu as pltpu
from jax.sharding import PartitionSpec as P

LANES = 128
ROWS = 8
TILE = LANES * ROWS


def plan(level, shift):
    if level == 0:
        return [0] * ROWS, 1
    half = ROWS >> level
    first, count = plan(level - 1, shift)
    second, _ = plan(level - 1, shift - half)
    owner = []
    for row in range(ROWS):
        keep = ((row - shift) // half) % 2 == 1
        owner.append(first[row] if keep else second[row] + count)
    return owner, 2 * count


PLACE, _ = plan(3, 0)


def fold(leaf, combine, rows, level=3, shift=0, first=0):
    if level == 0:
        return leaf(PLACE.index(first))
    half = ROWS >> level
    count = 1 << (level - 1)
    a = fold(leaf, combine, rows, level - 1, shift, first)
    b = fold(leaf, combine, rows, level - 1, shift - half, first + count)
    keep = (((rows - shift + 2 * ROWS) // half) % 2) == 1
    out = []
    for one, two, how in zip(a, b, combine, strict=True):
        mine = jnp.where(keep, one, two)
        other = jnp.where(keep, two, one)
        out.append(how(mine, pltpu.roll(other, half, 0)))
    return tuple(out)


def column(row, states):
    spread = jnp.broadcast_to(row, (states, states))
    eye = lax.broadcasted_iota(jnp.int32, (states, states), 0) == lax.broadcasted_iota(jnp.int32, (states, states), 1)
    picked = jnp.sum(jnp.where(eye, spread, 0.0), axis=1, keepdims=True)
    return jnp.broadcast_to(picked, (states, LANES))


def bases(counts_ref, free_ref, states):
    return column(jnp.log(counts_ref[...].astype(jnp.float32)) + free_ref[...], states)


def spot(flips):
    core = lax.axis_index("sample")
    flip = functools.reduce(lambda rest, c: jnp.where(core == c, flips[c], rest), range(1, len(flips)), flips[0])
    return jnp.bitwise_xor(jnp.bitwise_and(lax.axis_index("state"), 3), flip)


def over_tiles(x, how):
    parts = [x[i * ROWS : (i + 1) * ROWS] for i in range(x.shape[0] // ROWS)]
    return functools.reduce(how, parts)


def spread(x, g, states):
    return jnp.broadcast_to(x[g : g + 1, :], (states, LANES))


def sums_of(out_ref, energies_ref, offset, labels_ref, label_row, base, dirs, first_state, steps):
    states = energies_ref.shape[0]
    rows = lax.broadcasted_iota(jnp.int32, (ROWS, LANES), 0)
    ids = lax.broadcasted_iota(jnp.int32, (states, LANES), 0)

    def step(j, carry):
        at = pl.multiple_of(j * ROWS, ROWS)
        labels = labels_ref[pl.ds(pl.multiple_of(label_row + j * ROWS, ROWS), ROWS), :] - first_state

        def shifted(g):
            cols = pl.ds(pl.multiple_of(offset + j * TILE + g * LANES, LANES), LANES)
            return base[...] - energies_ref[:, cols]

        (peak,) = fold(lambda g: (over_tiles(shifted(g), jnp.maximum),), (jnp.maximum,), rows)

        def leaf(g):
            s = shifted(g)
            e = jnp.exp(s - spread(peak, g, states))
            return (
                over_tiles(e, jnp.add),
                over_tiles(e * dirs[0], jnp.add),
                over_tiles(e * dirs[1], jnp.add),
                over_tiles(jnp.where(ids == spread(labels, g, states), s, 0.0), jnp.add),
            )

        total, mix0, mix1, anchor = fold(leaf, (jnp.add,) * 4, rows)
        inverse = 1.0 / total
        out_ref[0, pl.ds(at, ROWS), :] = peak + jnp.log(total)
        out_ref[1, pl.ds(at, ROWS), :] = mix0 * inverse
        out_ref[2, pl.ds(at, ROWS), :] = mix1 * inverse
        out_ref[3, pl.ds(at, ROWS), :] = anchor
        return carry

    lax.fori_loop(0, steps, step, 0)


def first_body(flips, counts_hbm, free_hbm, dirs_hbm, labels_hbm, energies_hbm, *refs):
    out_ref, base_ref, dirs_ref, labels_ref, energies_ref, counts_s, free_s, dirs_s, sems = refs
    states, samples = energies_hbm.shape
    width = samples // 4
    pieces = sems.shape[0] - 7
    piece = width // pieces
    quarter = spot(flips)
    first_state = lax.axis_index("state") * states

    def energy_copy(start, size, sem):
        at = pl.ds(pl.multiple_of(start, size), size)
        return pltpu.make_async_copy(energies_hbm.at[:, at], energies_ref.at[:, at], sems.at[sem])

    small = [
        pltpu.make_async_copy(counts_hbm, counts_s, sems.at[0]),
        pltpu.make_async_copy(free_hbm, free_s, sems.at[1]),
        pltpu.make_async_copy(dirs_hbm, dirs_s, sems.at[2]),
        pltpu.make_async_copy(labels_hbm, labels_ref, sems.at[3]),
    ]
    near = [energy_copy(quarter * width + i * piece, piece, 7 + i) for i in range(pieces)]
    rest = [energy_copy(jnp.bitwise_xor(quarter, i) * width, width, 3 + i) for i in range(1, 4)]
    for copy in small + near + rest:
        copy.start()
    for copy in small:
        copy.wait()
    base_ref[...] = bases(counts_s, free_s, states)
    dirs_ref[0] = column(dirs_s[0:1, :], states)
    dirs_ref[1] = column(dirs_s[1:2, :], states)
    rows = piece // LANES
    for i, copy in enumerate(near):
        copy.wait()
        sums_of(
            out_ref.at[:, pl.ds(i * rows, rows), :],
            energies_ref,
            quarter * width + i * piece,
            labels_ref,
            quarter * (width // LANES) + i * rows,
            base_ref,
            dirs_ref,
            first_state,
            piece // TILE,
        )
    for copy in rest:
        copy.wait()


def later_body(flips, base_ref, dirs_ref, labels_ref, energies_ref, out_ref):
    states, samples = energies_ref.shape
    width = samples // 4
    quarter = spot(flips)
    first_state = lax.axis_index("state") * states
    offset, row = quarter * width, quarter * (width // LANES)
    sums_of(out_ref, energies_ref, offset, labels_ref, row, base_ref, dirs_ref, first_state, width // TILE)


def tally_body(labels_ref, tally_ref):
    states = tally_ref.shape[0]
    first_state = lax.axis_index("state") * states
    ids = lax.broadcasted_iota(jnp.int32, (states, LANES), 0)

    def step(j, tally):
        labels = labels_ref[pl.ds(pl.multiple_of(j * ROWS, ROWS), ROWS), :] - first_state
        for g in range(ROWS):
            tally += jnp.where(ids == spread(labels, g, states), 1.0, 0.0)
        return tally

    tally_ref[...] = lax.fori_loop(0, labels_ref.shape[0] // ROWS, step, jnp.zeros((states, LANES), jnp.float32))


def weigh(part_ref, energies_ref, quarter, base_ref):
    states, samples = energies_ref.shape
    width = samples // 4

    def step(j, carry):
        occupancy, mix0, mix1 = carry
        at = pl.ds(pl.multiple_of(j * ROWS, ROWS), ROWS)
        norm, first, second = part_ref[0, at, :], part_ref[1, at, :], part_ref[2, at, :]
        for g in range(ROWS):
            cols = pl.ds(pl.multiple_of(quarter * width + j * TILE + g * LANES, LANES), LANES)
            w = jnp.exp((base_ref[...] - energies_ref[:, cols]) - spread(norm, g, states))
            occupancy += w
            mix0 += w * spread(first, g, states)
            mix1 += w * spread(second, g, states)
        return occupancy, mix0, mix1

    zero = jnp.zeros((states, LANES), jnp.float32)
    return lax.fori_loop(0, width // TILE, step, (zero, zero, zero))


def weigh_body(flips, part_ref, base_ref, energies_ref, *refs):
    *before, sums_ref = refs
    for i, x in enumerate(weigh(part_ref, energies_ref, spot(flips), base_ref)):
        sums_ref[i] = x + before[0][i] if before else x


def last_body(flips, part_ref, base_ref, energies_ref, before_ref, dirs_ref, tally_ref, out_ref):
    sums = weigh(part_ref, energies_ref, spot(flips), base_ref)
    states = energies_ref.shape[0]
    eye = lax.broadcasted_iota(jnp.int32, (states, states), 0) == lax.broadcasted_iota(jnp.int32, (states, states), 1)

    def row(x):
        total = jnp.broadcast_to(jnp.sum(x, axis=1, keepdims=True), (states, states))
        return jnp.sum(jnp.where(eye, total, 0.0), axis=0, keepdims=True)

    occupancy = sums[0] + before_ref[0]
    out_ref[0:1, :] = row(occupancy - tally_ref[...])
    for j in range(2):
        out_ref[j + 1 : j + 2, :] = row(dirs_ref[j] * occupancy - (sums[j + 1] + before_ref[j + 1]))


def total_body(flips, scale, *refs):
    part_refs = refs[:4]
    mine_ref, other_ref, norm_hbm, anchor_hbm, gradient_hbm, products_hbm, gradient_s, products_s, sems = refs[4:]
    rows = norm_hbm.shape[0] // 4
    copies = []
    for k, part_ref in enumerate(part_refs):
        at = pl.ds(pl.multiple_of(spot(flips[k]) * rows, rows), rows)
        copies.append(pltpu.make_async_copy(part_ref.at[0], norm_hbm.at[at, :], sems.at[2 * k]))
        copies.append(pltpu.make_async_copy(part_ref.at[3], anchor_hbm.at[at, :], sems.at[2 * k + 1]))
    copies.append(pltpu.make_async_copy(gradient_s, gradient_hbm, sems.at[8]))
    copies.append(pltpu.make_async_copy(products_s, products_hbm, sems.at[9]))
    for copy in copies[:8]:
        copy.start()
    total = scale * (mine_ref[...] + other_ref[...])
    gradient_s[...] = total[0:1]
    products_s[...] = total[1:3]
    for copy in copies[8:]:
        copy.start()
    for copy in copies:
        copy.wait()


def merge_body(last, *refs):
    *parts, out_ref = refs
    norms = [part[0] for part in parts]
    peak = functools.reduce(jnp.maximum, norms)
    scales = [jnp.exp(norm - peak) for norm in norms]
    total = functools.reduce(jnp.add, scales)
    inverse = 1.0 / total
    norm = peak + jnp.log(total)
    anchor = functools.reduce(jnp.add, [part[3] for part in parts])
    out_ref[0] = norm
    for j in (1, 2):
        out_ref[j] = functools.reduce(jnp.add, [s * part[j] for s, part in zip(scales, parts, strict=True)]) * inverse
    out_ref[3] = anchor - norm if last else anchor


VMEM = pl.BlockSpec(memory_space=pltpu.VMEM)
HBM = pl.BlockSpec(memory_space=pltpu.HBM)
LIMIT = 16 * 1024 * 1024


def f32(*shape):
    return jax.ShapeDtypeStruct(shape, jnp.float32)


def kernel(body, in_specs, out_specs, out_shape, name, work, scratch=()):
    return pl.pallas_call(
        body,
        in_specs=in_specs,
        out_specs=out_specs,
        out_shape=out_shape,
        scratch_shapes=list(scratch),
        compiler_params=pltpu.CompilerParams(vmem_limit_bytes=LIMIT),
        cost_estimate=pl.CostEstimate(flops=work // 1024, bytes_accessed=1024, transcendentals=0),
        name=name,
    )


def swap(x, width, cores, flips):
    pairs = []
    for place in range(width):
        for core in range(cores):
            pairs.append((place * cores + core, (place ^ flips[core]) * cores + core))
    return lax.ppermute(x, ("state", "sample"), pairs)


def local(energies, counts, labels, free_energy, directions):
    states, samples = energies.shape
    width, cores = lax.axis_size("state"), lax.axis_size("sample")
    rounds = [(3,) * cores, tuple(1 + c % 2 for c in range(cores)), tuple(2 - c % 2 for c in range(cores))]
    stay = (0,) * cores
    rows = samples // 4 // LANES
    work = states * samples // 4
    labels = labels.reshape(samples // LANES, LANES)
    part = f32(4, rows, LANES)
    pieces = 2 if samples % (8 * TILE) == 0 else 1

    first, base, dirs, labels, energies = kernel(
        functools.partial(first_body, rounds[0]),
        [HBM] * 5,
        [VMEM] * 5,
        [
            part,
            f32(states, LANES),
            f32(2, states, LANES),
            jax.ShapeDtypeStruct(labels.shape, labels.dtype),
            f32(states, samples),
        ],
        "first_sums",
        work,
        [
            pltpu.VMEM((1, states), jnp.int32),
            pltpu.VMEM((1, states), jnp.float32),
            pltpu.VMEM((2, states), jnp.float32),
            pltpu.SemaphoreType.DMA((7 + pieces,)),
        ],
    )(
        *(
            pltpu.with_memory_space_constraint(x, pltpu.HBM)
            for x in (counts.reshape(1, states), free_energy.reshape(1, states), directions, labels, energies)
        )
    )

    def later(flips, name):
        return kernel(functools.partial(later_body, flips), [VMEM] * 4, VMEM, part, name, work)(
            base, dirs, labels, energies
        )

    def merge(parts, last, name):
        return kernel(functools.partial(merge_body, last), [VMEM] * len(parts), VMEM, part, name, 4 * rows * LANES)(
            *parts
        )

    def weigh_quarter(flips, x, before, name):
        args = [x, base, energies, *before]
        return kernel(
            functools.partial(weigh_body, flips), [VMEM] * len(args), VMEM, f32(3, states, LANES), name, work
        )(*args)

    sent = [first, later(rounds[1], "second_sums"), later(rounds[2], "third_sums")]
    got = [swap(x, width, cores, flips) for x, flips in zip(sent, rounds, strict=True)]
    own = later(stay, "own_sums")
    tally = kernel(tally_body, [VMEM], VMEM, f32(states, LANES), "tally", work)(labels)
    far = range(2, int(math.log2(width)))
    union = merge([own, got[0]], False, "merge_first")
    union = merge([union, got[1], got[2]], not far, "merge_square")
    for bit in far:
        union = merge([union, swap(union, width, cores, (1 << bit,) * cores)], bit == far[-1], "merge_far")
    others = [swap(union, width, cores, flips) for flips in rounds]
    sums = weigh_quarter(stay, union, [], "weigh_own")
    sums = weigh_quarter(rounds[0], others[0], [sums], "weigh_first")
    sums = weigh_quarter(rounds[1], others[1], [sums], "weigh_second")
    mine = kernel(
        functools.partial(last_body, rounds[2]), [VMEM] * 6, VMEM, f32(3, states), "last_sums", work
    )(others[2], base, energies, sums, dirs, tally)
    other = lax.ppermute(mine, "sample", [(c, cores - 1 - c) for c in range(cores)])
    long = f32(samples // LANES, LANES)
    log_norm, anchor_logp, gradient, products = kernel(
        functools.partial(total_body, (stay, *rounds), states * width / (samples * cores)),
        [VMEM] * 6,
        [HBM] * 4,
        [long, long, f32(1, states), f32(2, states)],
        "totals",
        1024,
        [pltpu.VMEM((1, states), jnp.float32), pltpu.VMEM((2, states), jnp.float32), pltpu.SemaphoreType.DMA((10,))],
    )(union, *others, mine, other)
    return log_norm.reshape(samples), anchor_logp.reshape(samples), gradient.reshape(states), products


def solution(mesh):
    return jax.shard_map(
        local,
        mesh=mesh,
        in_specs=(
            P(("group", "state"), "sample"),
            P(("group", "state")),
            P(("group", "sample")),
            P(("group", "state")),
            P(None, ("group", "state")),
        ),
        out_specs=(
            P(("group", "sample")),
            P(("group", "sample")),
            P(("group", "state")),
            P(None, ("group", "state")),
        ),
        check_vma=False,
    )
```

```python
import functools
import math

import jax
import jax.numpy as jnp
from jax import lax
from jax.experimental import pallas as pl
from jax.experimental.pallas import tpu as pltpu
from jax.sharding import PartitionSpec as P

LANES = 128
ROWS = 8
TILE = LANES * ROWS
CHUNKS = 1
FORWARD = True
RELAY = False


def plan(level, shift):
    if level == 0:
        return [0] * ROWS, 1
    half = ROWS >> level
    first, count = plan(level - 1, shift)
    second, _ = plan(level - 1, shift - half)
    owner = []
    for row in range(ROWS):
        keep = ((row - shift) // half) % 2 == 1
        owner.append(first[row] if keep else second[row] + count)
    return owner, 2 * count


PLACE, _ = plan(3, 0)


def fold(leaf, combine, rows, level=3, shift=0, first=0):
    if level == 0:
        return leaf(PLACE.index(first))
    half = ROWS >> level
    count = 1 << (level - 1)
    a = fold(leaf, combine, rows, level - 1, shift, first)
    b = fold(leaf, combine, rows, level - 1, shift - half, first + count)
    keep = (((rows - shift + 2 * ROWS) // half) % 2) == 1
    out = []
    for one, two, how in zip(a, b, combine, strict=True):
        mine = jnp.where(keep, one, two)
        other = jnp.where(keep, two, one)
        out.append(how(mine, pltpu.roll(other, half, 0)))
    return tuple(out)


def column(row, states):
    spread = jnp.broadcast_to(row, (states, states))
    eye = lax.broadcasted_iota(jnp.int32, (states, states), 0) == lax.broadcasted_iota(jnp.int32, (states, states), 1)
    picked = jnp.sum(jnp.where(eye, spread, 0.0), axis=1, keepdims=True)
    return jnp.broadcast_to(picked, (states, LANES))


def bases(counts_ref, free_ref, states):
    return column(jnp.log(counts_ref[...].astype(jnp.float32)) + free_ref[...], states)


def spot(flips):
    core = lax.axis_index("sample")
    flip = functools.reduce(lambda rest, c: jnp.where(core == c, flips[c], rest), range(1, len(flips)), flips[0])
    return jnp.bitwise_xor(jnp.bitwise_and(lax.axis_index("state"), 3), flip)


def over_tiles(x, how):
    parts = [x[i * ROWS : (i + 1) * ROWS] for i in range(x.shape[0] // ROWS)]
    return functools.reduce(how, parts)


def spread(x, g, states):
    return jnp.broadcast_to(x[g : g + 1, :], (states, LANES))


def sums_of(out_ref, energies_ref, offset, labels_ref, label_row, base, dirs, first_state, steps):
    states = energies_ref.shape[0]
    rows = lax.broadcasted_iota(jnp.int32, (ROWS, LANES), 0)
    ids = lax.broadcasted_iota(jnp.int32, (states, LANES), 0)

    def step(j, carry):
        at = pl.multiple_of(j * ROWS, ROWS)
        labels = labels_ref[pl.ds(pl.multiple_of(label_row + j * ROWS, ROWS), ROWS), :] - first_state

        def shifted(g):
            cols = pl.ds(pl.multiple_of(offset + j * TILE + g * LANES, LANES), LANES)
            return base[...] - energies_ref[:, cols]

        (peak,) = fold(lambda g: (over_tiles(shifted(g), jnp.maximum),), (jnp.maximum,), rows)

        def leaf(g):
            s = shifted(g)
            e = jnp.exp(s - spread(peak, g, states))
            return (
                over_tiles(e, jnp.add),
                over_tiles(e * dirs[0], jnp.add),
                over_tiles(e * dirs[1], jnp.add),
                over_tiles(jnp.where(ids == spread(labels, g, states), s, 0.0), jnp.add),
            )

        total, mix0, mix1, anchor = fold(leaf, (jnp.add,) * 4, rows)
        inverse = 1.0 / total
        out_ref[0, pl.ds(at, ROWS), :] = peak + jnp.log(total)
        out_ref[1, pl.ds(at, ROWS), :] = mix0 * inverse
        out_ref[2, pl.ds(at, ROWS), :] = mix1 * inverse
        out_ref[3, pl.ds(at, ROWS), :] = anchor
        return carry

    lax.fori_loop(0, steps, step, 0)


def first_body(flips, counts_hbm, free_hbm, dirs_hbm, labels_hbm, energies_hbm, *refs):
    out_ref, base_ref, dirs_ref, labels_ref, energies_ref, counts_s, free_s, dirs_s, sems = refs
    states, samples = energies_hbm.shape
    width = samples // 4
    size = out_ref.shape[1] * LANES
    pieces = sems.shape[0] - 8
    piece = size // pieces
    quarter = spot(flips)

    def energy_copy(start, size, sem):
        at = pl.ds(pl.multiple_of(start, LANES), size)
        return pltpu.make_async_copy(energies_hbm.at[:, at], energies_ref.at[:, at], sems.at[sem])

    small = [
        pltpu.make_async_copy(counts_hbm, counts_s, sems.at[0]),
        pltpu.make_async_copy(free_hbm, free_s, sems.at[1]),
        pltpu.make_async_copy(dirs_hbm, dirs_s, sems.at[2]),
        pltpu.make_async_copy(labels_hbm, labels_ref, sems.at[3]),
    ]
    near = [energy_copy(quarter * width + i * piece, piece, 8 + i) for i in range(pieces)]
    rest = [energy_copy(jnp.bitwise_xor(quarter, i) * width, width, 3 + i) for i in range(1, 4)]
    if size < width:
        rest.append(energy_copy(quarter * width + size, width - size, 7))
    for copy in small + near + rest:
        copy.start()
    for copy in small:
        copy.wait()
    base_ref[...] = bases(counts_s, free_s, states)
    dirs_ref[0] = column(dirs_s[0:1, :], states)
    dirs_ref[1] = column(dirs_s[1:2, :], states)
    rows = piece // LANES
    first_state = lax.axis_index("state") * states
    for i, copy in enumerate(near):
        copy.wait()
        sums_of(
            out_ref.at[:, pl.ds(i * rows, rows), :],
            energies_ref,
            quarter * width + i * piece,
            labels_ref,
            quarter * (width // LANES) + i * rows,
            base_ref,
            dirs_ref,
            first_state,
            piece // TILE,
        )
    for copy in rest:
        copy.wait()


def later_body(flips, chunk, base_ref, dirs_ref, labels_ref, energies_ref, out_ref):
    states, samples = energies_ref.shape
    width, rows = samples // 4, out_ref.shape[1]
    quarter = spot(flips)
    first_state = lax.axis_index("state") * states
    row = quarter * (width // LANES) + chunk * rows
    offset = quarter * width + chunk * rows * LANES
    sums_of(out_ref, energies_ref, offset, labels_ref, row, base_ref, dirs_ref, first_state, rows * LANES // TILE)


def tally_body(labels_ref, tally_ref):
    states = tally_ref.shape[0]
    first_state = lax.axis_index("state") * states
    ids = lax.broadcasted_iota(jnp.int32, (states, LANES), 0)

    def step(j, tally):
        labels = labels_ref[pl.ds(pl.multiple_of(j * ROWS, ROWS), ROWS), :] - first_state
        for g in range(ROWS):
            tally += jnp.where(ids == spread(labels, g, states), 1.0, 0.0)
        return tally

    tally_ref[...] = lax.fori_loop(0, labels_ref.shape[0] // ROWS, step, jnp.zeros((states, LANES), jnp.float32))


def weigh(part_ref, energies_ref, quarter, chunk, base_ref):
    states, samples = energies_ref.shape
    size = part_ref.shape[1] * LANES
    offset = quarter * (samples // 4) + chunk * size

    def step(j, carry):
        occupancy, mix0, mix1 = carry
        at = pl.ds(pl.multiple_of(j * ROWS, ROWS), ROWS)
        norm, first, second = part_ref[0, at, :], part_ref[1, at, :], part_ref[2, at, :]
        for g in range(ROWS):
            cols = pl.ds(pl.multiple_of(offset + j * TILE + g * LANES, LANES), LANES)
            w = jnp.exp((base_ref[...] - energies_ref[:, cols]) - spread(norm, g, states))
            occupancy += w
            mix0 += w * spread(first, g, states)
            mix1 += w * spread(second, g, states)
        return occupancy, mix0, mix1

    zero = jnp.zeros((states, LANES), jnp.float32)
    return lax.fori_loop(0, size // TILE, step, (zero, zero, zero))


def weigh_body(flips, chunk, part_ref, base_ref, energies_ref, *refs):
    *before, sums_ref = refs
    for i, x in enumerate(weigh(part_ref, energies_ref, spot(flips), chunk, base_ref)):
        sums_ref[i] = x + before[0][i] if before else x


def last_body(flips, chunk, part_ref, base_ref, energies_ref, dirs_ref, tally_ref, *refs):
    *before, out_ref = refs
    sums = list(weigh(part_ref, energies_ref, spot(flips), chunk, base_ref))
    for ref in before:
        sums = [x + ref[i] for i, x in enumerate(sums)]
    states = energies_ref.shape[0]
    eye = lax.broadcasted_iota(jnp.int32, (states, states), 0) == lax.broadcasted_iota(jnp.int32, (states, states), 1)

    def row(x):
        total = jnp.broadcast_to(jnp.sum(x, axis=1, keepdims=True), (states, states))
        return jnp.sum(jnp.where(eye, total, 0.0), axis=0, keepdims=True)

    out_ref[0:1, :] = row(sums[0] - tally_ref[...])
    for j in range(2):
        out_ref[j + 1 : j + 2, :] = row(dirs_ref[j] * sums[0] - sums[j + 1])


def total_body(flips, scale, *refs):
    *part_refs, mine_ref, other_ref, norm_hbm, anchor_hbm, gradient_hbm, products_hbm = refs[:-3]
    gradient_s, products_s, sems = refs[-3:]
    n = len(part_refs)
    rows = part_refs[0].shape[1]
    copies = []
    for k, part_ref in enumerate(part_refs):
        start = spot(flips[k // CHUNKS]) * (rows * CHUNKS) + (k % CHUNKS) * rows
        at = pl.ds(pl.multiple_of(start, ROWS), rows)
        copies.append(pltpu.make_async_copy(part_ref.at[0], norm_hbm.at[at, :], sems.at[2 * k]))
        copies.append(pltpu.make_async_copy(part_ref.at[3], anchor_hbm.at[at, :], sems.at[2 * k + 1]))
    copies.append(pltpu.make_async_copy(gradient_s, gradient_hbm, sems.at[2 * n]))
    copies.append(pltpu.make_async_copy(products_s, products_hbm, sems.at[2 * n + 1]))
    for copy in copies[: 2 * n]:
        copy.start()
    total = scale * (mine_ref[...] + other_ref[...])
    gradient_s[...] = total[0:1]
    products_s[...] = total[1:3]
    for copy in copies[2 * n :]:
        copy.start()
    for copy in copies:
        copy.wait()


def merge_body(last, *refs):
    *parts, out_ref = refs
    norms = [part[0] for part in parts]
    peak = functools.reduce(jnp.maximum, norms)
    scales = [jnp.exp(norm - peak) for norm in norms]
    total = functools.reduce(jnp.add, scales)
    inverse = 1.0 / total
    norm = peak + jnp.log(total)
    anchor = functools.reduce(jnp.add, [part[3] for part in parts])
    out_ref[0] = norm
    for j in (1, 2):
        out_ref[j] = functools.reduce(jnp.add, [s * part[j] for s, part in zip(scales, parts, strict=True)]) * inverse
    out_ref[3] = anchor - norm if last else anchor


VMEM = pl.BlockSpec(memory_space=pltpu.VMEM)
HBM = pl.BlockSpec(memory_space=pltpu.HBM)
LIMIT = 16 * 1024 * 1024


def f32(*shape):
    return jax.ShapeDtypeStruct(shape, jnp.float32)


def kernel(body, in_specs, out_specs, out_shape, name, work, scratch=()):
    return pl.pallas_call(
        body,
        in_specs=in_specs,
        out_specs=out_specs,
        out_shape=out_shape,
        scratch_shapes=list(scratch),
        compiler_params=pltpu.CompilerParams(vmem_limit_bytes=LIMIT),
        cost_estimate=pl.CostEstimate(flops=work // 1024, bytes_accessed=1024, transcendentals=0),
        name=name,
    )


def swap(x, width, cores, flips):
    pairs = []
    for place in range(width):
        for core in range(cores):
            pairs.append((place * cores + core, (place ^ flips[core]) * cores + core))
    return lax.ppermute(x, ("state", "sample"), pairs)


def local(energies, counts, labels, free_energy, directions):
    states, samples = energies.shape
    width, cores = lax.axis_size("state"), lax.axis_size("sample")
    near = tuple(1 + c % 2 for c in range(cores))
    side = tuple(2 - c % 2 for c in range(cores))
    across, stay = (3,) * cores, (0,) * cores
    rows = samples // 4 // LANES // CHUNKS
    work = states * rows * LANES
    labels = labels.reshape(samples // LANES, LANES)
    part = f32(4, rows, LANES)
    pieces = 2 if rows % (2 * ROWS) == 0 else 1

    first, base, dirs, labels, energies = kernel(
        functools.partial(first_body, across),
        [HBM] * 5,
        [VMEM] * 5,
        [
            part,
            f32(states, LANES),
            f32(2, states, LANES),
            jax.ShapeDtypeStruct(labels.shape, labels.dtype),
            f32(states, samples),
        ],
        "first_sums",
        work,
        [
            pltpu.VMEM((1, states), jnp.int32),
            pltpu.VMEM((1, states), jnp.float32),
            pltpu.VMEM((2, states), jnp.float32),
            pltpu.SemaphoreType.DMA((8 + pieces,)),
        ],
    )(
        *(
            pltpu.with_memory_space_constraint(x, pltpu.HBM)
            for x in (counts.reshape(1, states), free_energy.reshape(1, states), directions, labels, energies)
        )
    )

    def sums_for(flips, chunk, name):
        if chunk == 0 and flips == across:
            return first
        body = functools.partial(later_body, flips, chunk)
        return kernel(body, [VMEM] * 4, VMEM, part, f"{name}_{chunk}", work)(base, dirs, labels, energies)

    def merge(parts, last, name):
        return kernel(functools.partial(merge_body, last), [VMEM] * len(parts), VMEM, part, name, work)(*parts)

    def send(x, flips):
        return swap(x, width, cores, flips)

    def weigh_part(flips, chunk, x, before, name):
        args = [x, base, energies, *before]
        body = functools.partial(weigh_body, flips, chunk)
        return kernel(body, [VMEM] * len(args), VMEM, f32(3, states, LANES), f"{name}_{chunk}", work)(*args)

    far = range(2, int(math.log2(width)))
    tally = kernel(tally_body, [VMEM], VMEM, f32(states, LANES), "tally", work)(labels)
    found = []
    for chunk in range(CHUNKS):
        if FORWARD:
            got_side = send(sums_for(across, chunk, "across"), near)
            got = send(sums_for(near, chunk, "near"), near)
            pair = merge([sums_for(side, chunk, "side"), got_side], False, f"merge_side_{chunk}")
            union = merge([sums_for(stay, chunk, "own"), got], False, f"merge_near_{chunk}")
            union = merge([union, send(pair, side)], not far, f"merge_square_{chunk}")
        else:
            got = [send(sums_for(flips, chunk, f"sums{k}"), flips) for k, flips in enumerate((across, near, side))]
            union = merge([sums_for(stay, chunk, "own"), got[0]], False, f"merge_across_{chunk}")
            union = merge([union, got[1], got[2]], not far, f"merge_square_{chunk}")
        for bit in far:
            union = merge([union, send(union, (1 << bit,) * cores)], bit == far[-1], f"merge_far_{chunk}")
        if RELAY:
            from_side = send(union, side)
            found.append([(stay, union), (side, from_side), (near, send(union, near)), (across, send(from_side, near))])
        else:
            found.append([(stay, union)] + [(flips, send(union, flips)) for flips in (across, near, side)])
    sums = []
    for chunk, parts in enumerate(found):
        before = []
        for k, (flips, x) in enumerate(parts[:-1] if chunk == CHUNKS - 1 else parts):
            before = [weigh_part(flips, chunk, x, before, f"weigh{k}")]
        sums += before
    flips, x = found[-1][-1]
    body = functools.partial(last_body, flips, CHUNKS - 1)
    mine = kernel(body, [VMEM] * (5 + len(sums)), VMEM, f32(3, states), "last_sums", work)(
        x, base, energies, dirs, tally, *sums
    )
    other = lax.ppermute(mine, "sample", [(c, cores - 1 - c) for c in range(cores)])
    long = f32(samples // LANES, LANES)
    ends = [parts[k][1] for k in range(4) for parts in found]
    log_norm, anchor_logp, gradient, products = kernel(
        functools.partial(total_body, tuple(p[0] for p in found[0]), states * width / (samples * cores)),
        [VMEM] * (len(ends) + 2),
        [HBM] * 4,
        [long, long, f32(1, states), f32(2, states)],
        "totals",
        1024,
        [
            pltpu.VMEM((1, states), jnp.float32),
            pltpu.VMEM((2, states), jnp.float32),
            pltpu.SemaphoreType.DMA((2 * len(ends) + 2,)),
        ],
    )(*ends, mine, other)
    return log_norm.reshape(samples), anchor_logp.reshape(samples), gradient.reshape(states), products


def solution(mesh):
    return jax.shard_map(
        local,
        mesh=mesh,
        in_specs=(
            P(("group", "state"), "sample"),
            P(("group", "state")),
            P(("group", "sample")),
            P(("group", "state")),
            P(None, ("group", "state")),
        ),
        out_specs=(
            P(("group", "sample")),
            P(("group", "sample")),
            P(("group", "state")),
            P(None, ("group", "state")),
        ),
        check_vma=False,
    )
```

```python
import functools
import math

import jax
import jax.numpy as jnp
from jax import lax
from jax.experimental import pallas as pl
from jax.experimental.pallas import tpu as pltpu
from jax.sharding import PartitionSpec as P

LANES = 128
ROWS = 8
TILE = LANES * ROWS
LOADS = (2, 2)


def plan(level, shift):
    if level == 0:
        return [0] * ROWS, 1
    half = ROWS >> level
    first, count = plan(level - 1, shift)
    second, _ = plan(level - 1, shift - half)
    owner = []
    for row in range(ROWS):
        keep = ((row - shift) // half) % 2 == 1
        owner.append(first[row] if keep else second[row] + count)
    return owner, 2 * count


PLACE, _ = plan(3, 0)


def fold(leaf, combine, rows, level=3, shift=0, first=0):
    if level == 0:
        return leaf(PLACE.index(first))
    half = ROWS >> level
    count = 1 << (level - 1)
    a = fold(leaf, combine, rows, level - 1, shift, first)
    b = fold(leaf, combine, rows, level - 1, shift - half, first + count)
    keep = (((rows - shift + 2 * ROWS) // half) % 2) == 1
    out = []
    for one, two, how in zip(a, b, combine, strict=True):
        mine = jnp.where(keep, one, two)
        other = jnp.where(keep, two, one)
        out.append(how(mine, pltpu.roll(other, half, 0)))
    return tuple(out)


def column(row, states):
    spread = jnp.broadcast_to(row, (states, states))
    eye = lax.broadcasted_iota(jnp.int32, (states, states), 0) == lax.broadcasted_iota(jnp.int32, (states, states), 1)
    picked = jnp.sum(jnp.where(eye, spread, 0.0), axis=1, keepdims=True)
    return jnp.broadcast_to(picked, (states, LANES))


def bases(counts_ref, free_ref, states):
    return column(jnp.log(counts_ref[...].astype(jnp.float32)) + free_ref[...], states)


def spot(flip):
    return jnp.bitwise_xor(jnp.bitwise_and(lax.axis_index("state"), 3), flip)


def over_tiles(x, how):
    parts = [x[i * ROWS : (i + 1) * ROWS] for i in range(x.shape[0] // ROWS)]
    return functools.reduce(how, parts)


def spread(x, g, states):
    return jnp.broadcast_to(x[g : g + 1, :], (states, LANES))


def sums_of(out_ref, energies_ref, offset, labels_ref, label_row, base, dirs, steps):
    states = energies_ref.shape[0]
    rows = lax.broadcasted_iota(jnp.int32, (ROWS, LANES), 0)
    ids = lax.broadcasted_iota(jnp.int32, (states, LANES), 0)
    first_state = lax.axis_index("state") * states

    def step(j, carry):
        at = pl.multiple_of(j * ROWS, ROWS)
        labels = labels_ref[pl.ds(pl.multiple_of(label_row + j * ROWS, ROWS), ROWS), :] - first_state

        def shifted(g):
            cols = pl.ds(pl.multiple_of(offset + j * TILE + g * LANES, LANES), LANES)
            return base[...] - energies_ref[:, cols]

        (peak,) = fold(lambda g: (over_tiles(shifted(g), jnp.maximum),), (jnp.maximum,), rows)

        def leaf(g):
            s = shifted(g)
            e = jnp.exp(s - spread(peak, g, states))
            return (
                over_tiles(e, jnp.add),
                over_tiles(e * dirs[0], jnp.add),
                over_tiles(e * dirs[1], jnp.add),
                over_tiles(jnp.where(ids == spread(labels, g, states), s, 0.0), jnp.add),
            )

        total, mix0, mix1, anchor = fold(leaf, (jnp.add,) * 4, rows)
        inverse = 1.0 / total
        out_ref[0, pl.ds(at, ROWS), :] = peak + jnp.log(total)
        out_ref[1, pl.ds(at, ROWS), :] = mix0 * inverse
        out_ref[2, pl.ds(at, ROWS), :] = mix1 * inverse
        out_ref[3, pl.ds(at, ROWS), :] = anchor
        return carry

    lax.fori_loop(0, steps, step, 0)


def quarter_copies(flips, energies_hbm, quarter_refs, sems, first=0):
    width = quarter_refs[0].shape[1]
    copies = []
    for k, (flip, ref) in enumerate(zip(flips, quarter_refs, strict=True)):
        at = pl.ds(pl.multiple_of(spot(flip) * width, width), width)
        copies.append(pltpu.make_async_copy(energies_hbm.at[:, at], ref, sems.at[first + k]))
    return copies


def first_body(flips, pieces, counts_hbm, free_hbm, dirs_hbm, labels_hbm, energies_hbm, *refs):
    out_ref, base_ref, dirs_ref, labels_ref, near_ref, *rest_refs = refs[:-4]
    counts_s, free_s, dirs_s, sems = refs[-4:]
    states, width = near_ref.shape
    piece = width // pieces
    quarter = spot(flips[0])
    near = []
    for i in range(pieces):
        source = energies_hbm.at[:, pl.ds(pl.multiple_of(quarter * width + i * piece, piece), piece)]
        near.append(pltpu.make_async_copy(source, near_ref.at[:, pl.ds(i * piece, piece)], sems.at[i]))
    small = [
        pltpu.make_async_copy(counts_hbm, counts_s, sems.at[pieces]),
        pltpu.make_async_copy(free_hbm, free_s, sems.at[pieces + 1]),
        pltpu.make_async_copy(dirs_hbm, dirs_s, sems.at[pieces + 2]),
        pltpu.make_async_copy(labels_hbm, labels_ref, sems.at[pieces + 3]),
    ]
    rest = quarter_copies(flips[1:], energies_hbm, rest_refs, sems, pieces + 4) if rest_refs else []
    for copy in near[:1] + small + near[1:] + rest:
        copy.start()
    for copy in small:
        copy.wait()
    base_ref[...] = bases(counts_s, free_s, states)
    dirs_ref[0] = column(dirs_s[0:1, :], states)
    dirs_ref[1] = column(dirs_s[1:2, :], states)
    rows = piece // LANES
    for i, copy in enumerate(near):
        copy.wait()
        part = out_ref.at[:, pl.ds(i * rows, rows), :]
        row = quarter * (width // LANES) + i * rows
        sums_of(part, near_ref, i * piece, labels_ref, row, base_ref, dirs_ref, piece // TILE)
    for copy in rest:
        copy.wait()


def later_body(flip, loads, base_ref, dirs_ref, labels_ref, energies_ref, *refs):
    copies = []
    if loads:
        energies_hbm, out_ref, *load_refs, sems = refs
        copies = quarter_copies(loads, energies_hbm, load_refs, sems)
    else:
        (out_ref,) = refs
    for copy in copies:
        copy.start()
    width = energies_ref.shape[1]
    row = spot(flip) * (width // LANES)
    sums_of(out_ref, energies_ref, 0, labels_ref, row, base_ref, dirs_ref, width // TILE)
    for copy in copies:
        copy.wait()


def tally_body(labels_ref, tally_ref):
    states = tally_ref.shape[0]
    first_state = lax.axis_index("state") * states
    ids = lax.broadcasted_iota(jnp.int32, (states, LANES), 0)

    def step(j, tally):
        labels = labels_ref[pl.ds(pl.multiple_of(j * ROWS, ROWS), ROWS), :] - first_state
        for g in range(ROWS):
            tally += jnp.where(ids == spread(labels, g, states), 1.0, 0.0)
        return tally

    tally_ref[...] = lax.fori_loop(0, labels_ref.shape[0] // ROWS, step, jnp.zeros((states, LANES), jnp.float32))


def weigh(part_ref, energies_ref, base_ref):
    states, size = energies_ref.shape

    def step(j, carry):
        occupancy, mix0, mix1 = carry
        at = pl.ds(pl.multiple_of(j * ROWS, ROWS), ROWS)
        norm, first, second = part_ref[0, at, :], part_ref[1, at, :], part_ref[2, at, :]
        for g in range(ROWS):
            cols = pl.ds(pl.multiple_of(j * TILE + g * LANES, LANES), LANES)
            w = jnp.exp((base_ref[...] - energies_ref[:, cols]) - spread(norm, g, states))
            occupancy += w
            mix0 += w * spread(first, g, states)
            mix1 += w * spread(second, g, states)
        return occupancy, mix0, mix1

    zero = jnp.zeros((states, LANES), jnp.float32)
    return lax.fori_loop(0, size // TILE, step, (zero, zero, zero))


def weigh_body(part_ref, base_ref, energies_ref, *refs):
    *before, sums_ref = refs
    for i, x in enumerate(weigh(part_ref, energies_ref, base_ref)):
        sums_ref[i] = x + before[0][i] if before else x


def last_body(part_ref, base_ref, energies_ref, dirs_ref, tally_ref, before_ref, out_ref):
    sums = [x + before_ref[i] for i, x in enumerate(weigh(part_ref, energies_ref, base_ref))]
    states = energies_ref.shape[0]
    eye = lax.broadcasted_iota(jnp.int32, (states, states), 0) == lax.broadcasted_iota(jnp.int32, (states, states), 1)

    def row(x):
        total = jnp.broadcast_to(jnp.sum(x, axis=1, keepdims=True), (states, states))
        return jnp.sum(jnp.where(eye, total, 0.0), axis=0, keepdims=True)

    out_ref[0:1, :] = row(sums[0] - tally_ref[...])
    for j in range(2):
        out_ref[j + 1 : j + 2, :] = row(dirs_ref[j] * sums[0] - sums[j + 1])


def total_body(flips, scale, *refs):
    *part_refs, mine_ref, other_ref, norm_hbm, anchor_hbm, gradient_hbm, products_hbm = refs[:-3]
    gradient_s, products_s, sems = refs[-3:]
    n = len(part_refs)
    rows = part_refs[0].shape[1]
    copies = []
    for k, part_ref in enumerate(part_refs):
        at = pl.ds(pl.multiple_of(spot(flips[k]) * rows, rows), rows)
        copies.append(pltpu.make_async_copy(part_ref.at[0], norm_hbm.at[at, :], sems.at[2 * k]))
        copies.append(pltpu.make_async_copy(part_ref.at[3], anchor_hbm.at[at, :], sems.at[2 * k + 1]))
    copies.append(pltpu.make_async_copy(gradient_s, gradient_hbm, sems.at[2 * n]))
    copies.append(pltpu.make_async_copy(products_s, products_hbm, sems.at[2 * n + 1]))
    for copy in copies[: 2 * n]:
        copy.start()
    total = scale * (mine_ref[...] + other_ref[...])
    gradient_s[...] = total[0:1]
    products_s[...] = total[1:3]
    for copy in copies[2 * n :]:
        copy.start()
    for copy in copies:
        copy.wait()


def unite(parts, out_ref, last=False):
    norms = [part[0] for part in parts]
    peak = functools.reduce(jnp.maximum, norms)
    scales = [jnp.exp(norm - peak) for norm in norms]
    total = functools.reduce(jnp.add, scales)
    inverse = 1.0 / total
    norm = peak + jnp.log(total)
    anchor = functools.reduce(jnp.add, [part[3] for part in parts])
    out_ref[0] = norm
    for j in (1, 2):
        out_ref[j] = functools.reduce(jnp.add, [s * part[j] for s, part in zip(scales, parts, strict=True)]) * inverse
    out_ref[3] = anchor - norm if last else anchor


def merge_body(last, *refs):
    unite(refs[:-1], refs[-1], last)


VMEM = pl.BlockSpec(memory_space=pltpu.VMEM)
HBM = pl.BlockSpec(memory_space=pltpu.HBM)
LIMIT = 16 * 1024 * 1024


def f32(*shape):
    return jax.ShapeDtypeStruct(shape, jnp.float32)


def kernel(body, in_specs, out_specs, out_shape, name, work, scratch=()):
    return pl.pallas_call(
        body,
        in_specs=in_specs,
        out_specs=out_specs,
        out_shape=out_shape,
        scratch_shapes=list(scratch),
        compiler_params=pltpu.CompilerParams(vmem_limit_bytes=LIMIT),
        cost_estimate=pl.CostEstimate(flops=work // 1024, bytes_accessed=1024, transcendentals=0),
        name=name,
    )


def local(energies, counts, labels, free_energy, directions):
    states, samples = energies.shape
    width, cores = lax.axis_size("state"), lax.axis_size("sample")
    near, side, across, stay = 2, 1, 3, 0
    order, loads = (across, near, side, stay), LOADS
    rows = samples // 4 // LANES
    work = states * rows * LANES
    labels_in = labels.reshape(samples // LANES, LANES)
    part = f32(4, rows, LANES)
    pieces = 8 if rows % (8 * ROWS) == 0 else 1
    quarter = f32(states, samples // 4)
    energies = pltpu.with_memory_space_constraint(energies, pltpu.HBM)

    first, base, dirs, labels, *quarters = kernel(
        functools.partial(first_body, order[: loads[0]], pieces),
        [HBM] * 5,
        [VMEM] * (4 + loads[0]),
        [
            part,
            f32(states, LANES),
            f32(2, states, LANES),
            jax.ShapeDtypeStruct(labels_in.shape, labels_in.dtype),
        ]
        + [quarter] * loads[0],
        "first_sums",
        work,
        [
            pltpu.VMEM((1, states), jnp.int32),
            pltpu.VMEM((1, states), jnp.float32),
            pltpu.VMEM((2, states), jnp.float32),
            pltpu.SemaphoreType.DMA((pieces + 3 + loads[0],)),
        ],
    )(
        *(
            pltpu.with_memory_space_constraint(x, pltpu.HBM)
            for x in (counts.reshape(1, states), free_energy.reshape(1, states), directions, labels_in)
        ),
        energies,
    )

    def sums_for(k, name):
        have = len(quarters)
        more = order[have : have + (loads[k] if k < len(loads) else 0)]
        out, *loaded = kernel(
            functools.partial(later_body, order[k], more),
            [VMEM] * 4 + [HBM] * bool(more),
            [VMEM] * (1 + len(more)),
            [part] + [quarter] * len(more),
            name,
            work,
            [pltpu.SemaphoreType.DMA((len(more),))] if more else [],
        )(base, dirs, labels, quarters[k], *([energies] if more else []))
        quarters.extend(loaded)
        return out

    def send(x, flip):
        return lax.ppermute(x, "state", [(place, place ^ flip) for place in range(width)])

    def weigh_part(k, x, before, name):
        args = [x, base, quarters[k], *before]
        return kernel(weigh_body, [VMEM] * len(args), VMEM, f32(3, states, LANES), name, work)(*args)

    def merge(parts, last, name):
        return kernel(functools.partial(merge_body, last), [VMEM] * len(parts), VMEM, part, name, work)(*parts)

    far = range(2, int(math.log2(width)))
    got_side = send(first, near)
    got_near = send(sums_for(1, "near_sums"), near)
    pair = merge([sums_for(2, "side_sums"), got_side], False, "merge_pair")
    got_pair = send(pair, side)
    union = merge([sums_for(3, "own_sums"), got_near], False, "merge_near")
    union = merge([union, got_pair], not far, "merge_square")
    tally = kernel(tally_body, [VMEM], VMEM, f32(states, LANES), "tally", work)(labels)
    for bit in far:
        union = merge([union, send(union, 1 << bit)], bit == far[-1], "merge_far")
    ends = [(3, union)] + [(k, send(union, order[k])) for k in range(3)]
    sums = []
    for k, x in ends[:-1]:
        sums = [weigh_part(k, x, sums, f"weigh{k}")]
    k, x = ends[-1]
    mine = kernel(last_body, [VMEM] * 6, VMEM, f32(3, states), "last_sums", work)(
        x, base, quarters[k], dirs, tally, *sums
    )
    other = lax.ppermute(mine, "sample", [(c, cores - 1 - c) for c in range(cores)])
    long = f32(samples // LANES, LANES)
    log_norm, anchor_logp, gradient, products = kernel(
        functools.partial(total_body, tuple(order[k] for k, _ in ends), states * width / (samples * cores)),
        [VMEM] * (len(ends) + 2),
        [HBM] * 4,
        [long, long, f32(1, states), f32(2, states)],
        "totals",
        1024,
        [
            pltpu.VMEM((1, states), jnp.float32),
            pltpu.VMEM((2, states), jnp.float32),
            pltpu.SemaphoreType.DMA((2 * len(ends) + 2,)),
        ],
    )(*(x for _, x in ends), mine, other)
    return log_norm.reshape(samples), anchor_logp.reshape(samples), gradient.reshape(states), products


def solution(mesh):
    return jax.shard_map(
        local,
        mesh=mesh,
        in_specs=(
            P(("group", "state"), "sample"),
            P(("group", "state")),
            P(("group", "sample")),
            P(("group", "state")),
            P(None, ("group", "state")),
        ),
        out_specs=(
            P(("group", "sample")),
            P(("group", "sample")),
            P(("group", "state")),
            P(None, ("group", "state")),
        ),
        check_vma=False,
    )
```

```python
import functools
import math

import jax
import jax.numpy as jnp
from jax import lax
from jax.experimental import pallas as pl
from jax.experimental.pallas import tpu as pltpu
from jax.sharding import PartitionSpec as P

LANES = 128
ROWS = 8
TILE = LANES * ROWS
LOADS = (1, 3)


def plan(level, shift):
    if level == 0:
        return [0] * ROWS, 1
    half = ROWS >> level
    first, count = plan(level - 1, shift)
    second, _ = plan(level - 1, shift - half)
    owner = []
    for row in range(ROWS):
        keep = ((row - shift) // half) % 2 == 1
        owner.append(first[row] if keep else second[row] + count)
    return owner, 2 * count


PLACE, _ = plan(3, 0)


def fold(leaf, combine, rows, level=3, shift=0, first=0):
    if level == 0:
        return leaf(PLACE.index(first))
    half = ROWS >> level
    count = 1 << (level - 1)
    a = fold(leaf, combine, rows, level - 1, shift, first)
    b = fold(leaf, combine, rows, level - 1, shift - half, first + count)
    keep = (((rows - shift + 2 * ROWS) // half) % 2) == 1
    out = []
    for one, two, how in zip(a, b, combine, strict=True):
        mine = jnp.where(keep, one, two)
        other = jnp.where(keep, two, one)
        out.append(how(mine, pltpu.roll(other, half, 0)))
    return tuple(out)


def column(row, states):
    spread = jnp.broadcast_to(row, (states, states))
    eye = lax.broadcasted_iota(jnp.int32, (states, states), 0) == lax.broadcasted_iota(jnp.int32, (states, states), 1)
    picked = jnp.sum(jnp.where(eye, spread, 0.0), axis=1, keepdims=True)
    return jnp.broadcast_to(picked, (states, LANES))


def bases(counts_ref, free_ref, states):
    return column(jnp.log(counts_ref[...].astype(jnp.float32)) + free_ref[...], states)


def spot(flip):
    return jnp.bitwise_xor(jnp.bitwise_and(lax.axis_index("state"), 3), flip)


def over_tiles(x, how):
    parts = [x[i * ROWS : (i + 1) * ROWS] for i in range(x.shape[0] // ROWS)]
    return functools.reduce(how, parts)


def spread(x, g, states):
    return jnp.broadcast_to(x[g : g + 1, :], (states, LANES))


def sums_of(out_ref, energies_ref, offset, labels_ref, label_row, base, dirs, steps):
    states = energies_ref.shape[0]
    rows = lax.broadcasted_iota(jnp.int32, (ROWS, LANES), 0)
    ids = lax.broadcasted_iota(jnp.int32, (states, LANES), 0)
    first_state = lax.axis_index("state") * states

    def step(j, carry):
        at = pl.multiple_of(j * ROWS, ROWS)
        labels = labels_ref[pl.ds(pl.multiple_of(label_row + j * ROWS, ROWS), ROWS), :] - first_state

        def shifted(g):
            cols = pl.ds(pl.multiple_of(offset + j * TILE + g * LANES, LANES), LANES)
            return base[...] - energies_ref[:, cols]

        (peak,) = fold(lambda g: (over_tiles(shifted(g), jnp.maximum),), (jnp.maximum,), rows)

        def leaf(g):
            s = shifted(g)
            e = jnp.exp(s - spread(peak, g, states))
            return (
                over_tiles(e, jnp.add),
                over_tiles(e * dirs[0], jnp.add),
                over_tiles(e * dirs[1], jnp.add),
                over_tiles(jnp.where(ids == spread(labels, g, states), s, 0.0), jnp.add),
            )

        total, mix0, mix1, anchor = fold(leaf, (jnp.add,) * 4, rows)
        inverse = 1.0 / total
        out_ref[0, pl.ds(at, ROWS), :] = peak + jnp.log(total)
        out_ref[1, pl.ds(at, ROWS), :] = mix0 * inverse
        out_ref[2, pl.ds(at, ROWS), :] = mix1 * inverse
        out_ref[3, pl.ds(at, ROWS), :] = anchor
        return carry

    lax.fori_loop(0, steps, step, 0)


def quarter_copy(flip, energies_hbm, quarter_ref, pieces):
    width = quarter_ref.shape[1]
    size = width // len(pieces)
    copies = []
    for i, sem in enumerate(pieces):
        source = energies_hbm.at[:, pl.ds(pl.multiple_of(spot(flip) * width + i * size, size), size)]
        copies.append(pltpu.make_async_copy(source, quarter_ref.at[:, pl.ds(i * size, size)], sem))
    return copies


def piecewise(flip, copies, out_ref, quarter_ref, labels_ref, base_ref, dirs_ref):
    width = quarter_ref.shape[1]
    n = max(len(copies), 1)
    size, rows = width // n, width // LANES // n
    for i in range(n):
        if copies:
            copies[i].wait()
        part = out_ref.at[:, pl.ds(i * rows, rows), :]
        row = spot(flip) * (width // LANES) + i * rows
        sums_of(part, quarter_ref, i * size, labels_ref, row, base_ref, dirs_ref, size // TILE)


def first_body(flips, pieces, counts_hbm, free_hbm, dirs_hbm, labels_hbm, energies_hbm, *refs):
    out_ref, base_ref, dirs_ref, labels_ref, *quarter_refs = refs[:-4]
    counts_s, free_s, dirs_s, sems = refs[-4:]
    states = base_ref.shape[0]
    own = quarter_copy(flips[0], energies_hbm, quarter_refs[0], [sems.at[i] for i in range(pieces)])
    small = [
        pltpu.make_async_copy(counts_hbm, counts_s, sems.at[pieces]),
        pltpu.make_async_copy(free_hbm, free_s, sems.at[pieces + 1]),
        pltpu.make_async_copy(dirs_hbm, dirs_s, sems.at[pieces + 2]),
    ]
    rows = labels_ref.shape[0] // 4
    marks = []
    for i in range(4):
        at = pl.ds(pl.multiple_of(jnp.bitwise_xor(spot(flips[0]), i) * rows, rows), rows)
        marks.append(pltpu.make_async_copy(labels_hbm.at[at, :], labels_ref.at[at, :], sems.at[pieces + 3 + i]))
    rest = []
    for k in range(1, len(flips)):
        rest += quarter_copy(flips[k], energies_hbm, quarter_refs[k], [sems.at[pieces + 6 + k]])
    for copy in small + own[:1] + marks[:1] + own[1:] + marks[1:] + rest:
        copy.start()
    for copy in small:
        copy.wait()
    base_ref[...] = bases(counts_s, free_s, states)
    dirs_ref[0] = column(dirs_s[0:1, :], states)
    dirs_ref[1] = column(dirs_s[1:2, :], states)
    marks[0].wait()
    piecewise(flips[0], own, out_ref, quarter_refs[0], labels_ref, base_ref, dirs_ref)
    for copy in marks[1:] + rest:
        copy.wait()


def later_body(flip, loads, pieces, base_ref, dirs_ref, labels_ref, *refs):
    own, rest = [], []
    if loads:
        energies_hbm, out_ref, *load_refs, sems = refs[-3 - len(loads) :]
        for k, (load, ref) in enumerate(zip(loads, load_refs, strict=True)):
            if load == flip:
                own = quarter_copy(load, energies_hbm, ref, [sems.at[len(loads) + i] for i in range(pieces)])
            else:
                rest += quarter_copy(load, energies_hbm, ref, [sems.at[k]])
        quarter_ref = load_refs[0] if own else refs[0]
    else:
        quarter_ref, out_ref = refs
    for copy in own + rest:
        copy.start()
    piecewise(flip, own, out_ref, quarter_ref, labels_ref, base_ref, dirs_ref)
    for copy in rest:
        copy.wait()


def tally_body(labels_ref, tally_ref):
    states = tally_ref.shape[0]
    first_state = lax.axis_index("state") * states
    ids = lax.broadcasted_iota(jnp.int32, (states, LANES), 0)

    def step(j, tally):
        labels = labels_ref[pl.ds(pl.multiple_of(j * ROWS, ROWS), ROWS), :] - first_state
        for g in range(ROWS):
            tally += jnp.where(ids == spread(labels, g, states), 1.0, 0.0)
        return tally

    tally_ref[...] = lax.fori_loop(0, labels_ref.shape[0] // ROWS, step, jnp.zeros((states, LANES), jnp.float32))


def weigh(part_ref, energies_ref, base_ref):
    states, size = energies_ref.shape

    def step(j, carry):
        occupancy, mix0, mix1 = carry
        at = pl.ds(pl.multiple_of(j * ROWS, ROWS), ROWS)
        norm, first, second = part_ref[0, at, :], part_ref[1, at, :], part_ref[2, at, :]
        for g in range(ROWS):
            cols = pl.ds(pl.multiple_of(j * TILE + g * LANES, LANES), LANES)
            w = jnp.exp((base_ref[...] - energies_ref[:, cols]) - spread(norm, g, states))
            occupancy += w
            mix0 += w * spread(first, g, states)
            mix1 += w * spread(second, g, states)
        return occupancy, mix0, mix1

    zero = jnp.zeros((states, LANES), jnp.float32)
    return lax.fori_loop(0, size // TILE, step, (zero, zero, zero))


def weigh_body(part_ref, base_ref, energies_ref, *refs):
    *before, sums_ref = refs
    for i, x in enumerate(weigh(part_ref, energies_ref, base_ref)):
        sums_ref[i] = x + before[0][i] if before else x


def last_body(part_ref, base_ref, energies_ref, dirs_ref, tally_ref, before_ref, out_ref):
    sums = [x + before_ref[i] for i, x in enumerate(weigh(part_ref, energies_ref, base_ref))]
    states = energies_ref.shape[0]
    eye = lax.broadcasted_iota(jnp.int32, (states, states), 0) == lax.broadcasted_iota(jnp.int32, (states, states), 1)

    def row(x):
        total = jnp.broadcast_to(jnp.sum(x, axis=1, keepdims=True), (states, states))
        return jnp.sum(jnp.where(eye, total, 0.0), axis=0, keepdims=True)

    out_ref[0:1, :] = row(sums[0] - tally_ref[...])
    for j in range(2):
        out_ref[j + 1 : j + 2, :] = row(dirs_ref[j] * sums[0] - sums[j + 1])


def total_body(flips, scale, *refs):
    *part_refs, mine_ref, other_ref, norm_hbm, anchor_hbm, gradient_hbm, products_hbm = refs[:-3]
    gradient_s, products_s, sems = refs[-3:]
    n = len(part_refs)
    rows = part_refs[0].shape[1]
    copies = []
    for k, part_ref in enumerate(part_refs):
        at = pl.ds(pl.multiple_of(spot(flips[k]) * rows, rows), rows)
        copies.append(pltpu.make_async_copy(part_ref.at[0], norm_hbm.at[at, :], sems.at[2 * k]))
        copies.append(pltpu.make_async_copy(part_ref.at[3], anchor_hbm.at[at, :], sems.at[2 * k + 1]))
    copies.append(pltpu.make_async_copy(gradient_s, gradient_hbm, sems.at[2 * n]))
    copies.append(pltpu.make_async_copy(products_s, products_hbm, sems.at[2 * n + 1]))
    for copy in copies[: 2 * n]:
        copy.start()
    total = scale * (mine_ref[...] + other_ref[...])
    gradient_s[...] = total[0:1]
    products_s[...] = total[1:3]
    for copy in copies[2 * n :]:
        copy.start()
    for copy in copies:
        copy.wait()


def unite(parts, out_ref, last=False):
    norms = [part[0] for part in parts]
    peak = functools.reduce(jnp.maximum, norms)
    scales = [jnp.exp(norm - peak) for norm in norms]
    total = functools.reduce(jnp.add, scales)
    inverse = 1.0 / total
    norm = peak + jnp.log(total)
    anchor = functools.reduce(jnp.add, [part[3] for part in parts])
    out_ref[0] = norm
    for j in (1, 2):
        out_ref[j] = functools.reduce(jnp.add, [s * part[j] for s, part in zip(scales, parts, strict=True)]) * inverse
    out_ref[3] = anchor - norm if last else anchor


def merge_body(last, *refs):
    unite(refs[:-1], refs[-1], last)


VMEM = pl.BlockSpec(memory_space=pltpu.VMEM)
HBM = pl.BlockSpec(memory_space=pltpu.HBM)
LIMIT = 16 * 1024 * 1024


def f32(*shape):
    return jax.ShapeDtypeStruct(shape, jnp.float32)


def kernel(body, in_specs, out_specs, out_shape, name, work, scratch=()):
    return pl.pallas_call(
        body,
        in_specs=in_specs,
        out_specs=out_specs,
        out_shape=out_shape,
        scratch_shapes=list(scratch),
        compiler_params=pltpu.CompilerParams(vmem_limit_bytes=LIMIT),
        cost_estimate=pl.CostEstimate(flops=work // 1024, bytes_accessed=1024, transcendentals=0),
        name=name,
    )


def local(energies, counts, labels, free_energy, directions):
    states, samples = energies.shape
    width, cores = lax.axis_size("state"), lax.axis_size("sample")
    near, side, across, stay = 2, 1, 3, 0
    order, loads = (across, near, side, stay), LOADS
    rows = samples // 4 // LANES
    work = states * rows * LANES
    labels_in = labels.reshape(samples // LANES, LANES)
    part = f32(4, rows, LANES)
    pieces = 8 if rows % (8 * ROWS) == 0 else 1
    quarter = f32(states, samples // 4)
    energies = pltpu.with_memory_space_constraint(energies, pltpu.HBM)

    first, base, dirs, labels, *quarters = kernel(
        functools.partial(first_body, order[: loads[0]], pieces),
        [HBM] * 5,
        [VMEM] * (4 + loads[0]),
        [
            part,
            f32(states, LANES),
            f32(2, states, LANES),
            jax.ShapeDtypeStruct(labels_in.shape, labels_in.dtype),
        ]
        + [quarter] * loads[0],
        "first_sums",
        work,
        [
            pltpu.VMEM((1, states), jnp.int32),
            pltpu.VMEM((1, states), jnp.float32),
            pltpu.VMEM((2, states), jnp.float32),
            pltpu.SemaphoreType.DMA((pieces + 6 + loads[0],)),
        ],
    )(
        *(
            pltpu.with_memory_space_constraint(x, pltpu.HBM)
            for x in (counts.reshape(1, states), free_energy.reshape(1, states), directions, labels_in)
        ),
        energies,
    )

    def sums_for(k, name):
        have = len(quarters)
        more = order[have : have + (loads[k] if k < len(loads) else 0)]
        args = [base, dirs, labels] + ([quarters[k]] if k < have else []) + ([energies] if more else [])
        out, *loaded = kernel(
            functools.partial(later_body, order[k], more, pieces),
            [VMEM] * (len(args) - bool(more)) + [HBM] * bool(more),
            [VMEM] * (1 + len(more)),
            [part] + [quarter] * len(more),
            name,
            work,
            [pltpu.SemaphoreType.DMA((len(more) + pieces,))] if more else [],
        )(*args)
        quarters.extend(loaded)
        return out

    def send(x, flip):
        return lax.ppermute(x, "state", [(place, place ^ flip) for place in range(width)])

    def weigh_part(k, x, before, name):
        args = [x, base, quarters[k], *before]
        return kernel(weigh_body, [VMEM] * len(args), VMEM, f32(3, states, LANES), name, work)(*args)

    def merge(parts, last, name):
        return kernel(functools.partial(merge_body, last), [VMEM] * len(parts), VMEM, part, name, work)(*parts)

    far = range(2, int(math.log2(width)))
    got_side = send(first, near)
    got_near = send(sums_for(1, "near_sums"), near)
    pair = merge([sums_for(2, "side_sums"), got_side], False, "merge_pair")
    got_pair = send(pair, side)
    union = merge([sums_for(3, "own_sums"), got_near], False, "merge_near")
    union = merge([union, got_pair], not far, "merge_square")
    tally = kernel(tally_body, [VMEM], VMEM, f32(states, LANES), "tally", work)(labels)
    for bit in far:
        union = merge([union, send(union, 1 << bit)], bit == far[-1], "merge_far")
    ends = [(3, union)] + [(k, send(union, order[k])) for k in range(3)]
    sums = []
    for k, x in ends[:-1]:
        sums = [weigh_part(k, x, sums, f"weigh{k}")]
    k, x = ends[-1]
    mine = kernel(last_body, [VMEM] * 6, VMEM, f32(3, states), "last_sums", work)(
        x, base, quarters[k], dirs, tally, *sums
    )
    other = lax.ppermute(mine, "sample", [(c, cores - 1 - c) for c in range(cores)])
    long = f32(samples // LANES, LANES)
    log_norm, anchor_logp, gradient, products = kernel(
        functools.partial(total_body, tuple(order[k] for k, _ in ends), states * width / (samples * cores)),
        [VMEM] * (len(ends) + 2),
        [HBM] * 4,
        [long, long, f32(1, states), f32(2, states)],
        "totals",
        1024,
        [
            pltpu.VMEM((1, states), jnp.float32),
            pltpu.VMEM((2, states), jnp.float32),
            pltpu.SemaphoreType.DMA((2 * len(ends) + 2,)),
        ],
    )(*(x for _, x in ends), mine, other)
    return log_norm.reshape(samples), anchor_logp.reshape(samples), gradient.reshape(states), products


def solution(mesh):
    return jax.shard_map(
        local,
        mesh=mesh,
        in_specs=(
            P(("group", "state"), "sample"),
            P(("group", "state")),
            P(("group", "sample")),
            P(("group", "state")),
            P(None, ("group", "state")),
        ),
        out_specs=(
            P(("group", "sample")),
            P(("group", "sample")),
            P(("group", "state")),
            P(None, ("group", "state")),
        ),
        check_vma=False,
    )
```

```python
import functools
import math

import jax
import jax.numpy as jnp
from jax import lax
from jax.experimental import pallas as pl
from jax.experimental.pallas import tpu as pltpu
from jax.sharding import PartitionSpec as P

LANES = 128
ROWS = 8
TILE = LANES * ROWS
LOADS = (1, 3)


def plan(level, shift):
    if level == 0:
        return [0] * ROWS, 1
    half = ROWS >> level
    first, count = plan(level - 1, shift)
    second, _ = plan(level - 1, shift - half)
    owner = []
    for row in range(ROWS):
        keep = ((row - shift) // half) % 2 == 1
        owner.append(first[row] if keep else second[row] + count)
    return owner, 2 * count


PLACE, _ = plan(3, 0)


def fold(leaf, combine, rows, level=3, shift=0, first=0):
    if level == 0:
        return leaf(PLACE.index(first))
    half = ROWS >> level
    count = 1 << (level - 1)
    a = fold(leaf, combine, rows, level - 1, shift, first)
    b = fold(leaf, combine, rows, level - 1, shift - half, first + count)
    keep = (((rows - shift + 2 * ROWS) // half) % 2) == 1
    out = []
    for one, two, how in zip(a, b, combine, strict=True):
        mine = jnp.where(keep, one, two)
        other = jnp.where(keep, two, one)
        out.append(how(mine, pltpu.roll(other, half, 0)))
    return tuple(out)


def column(row, states):
    spread = jnp.broadcast_to(row, (states, states))
    eye = lax.broadcasted_iota(jnp.int32, (states, states), 0) == lax.broadcasted_iota(jnp.int32, (states, states), 1)
    picked = jnp.sum(jnp.where(eye, spread, 0.0), axis=1, keepdims=True)
    return jnp.broadcast_to(picked, (states, LANES))


def bases(counts_ref, free_ref, states):
    return column(jnp.log(counts_ref[...].astype(jnp.float32)) + free_ref[...], states)


def spot(flip):
    return jnp.bitwise_xor(jnp.bitwise_and(lax.axis_index("state"), 3), flip)


def over_tiles(x, how):
    parts = [x[i * ROWS : (i + 1) * ROWS] for i in range(x.shape[0] // ROWS)]
    return functools.reduce(how, parts)


def spread(x, g, states):
    return jnp.broadcast_to(x[g : g + 1, :], (states, LANES))


def sums_of(out_ref, energies_ref, offset, labels_ref, label_row, base, dirs, steps):
    states = energies_ref.shape[0]
    rows = lax.broadcasted_iota(jnp.int32, (ROWS, LANES), 0)
    ids = lax.broadcasted_iota(jnp.int32, (states, LANES), 0)
    first_state = lax.axis_index("state") * states

    def step(j, carry):
        at = pl.multiple_of(j * ROWS, ROWS)
        labels = labels_ref[pl.ds(pl.multiple_of(label_row + j * ROWS, ROWS), ROWS), :] - first_state

        def shifted(g):
            cols = pl.ds(pl.multiple_of(offset + j * TILE + g * LANES, LANES), LANES)
            return base[...] - energies_ref[:, cols]

        (peak,) = fold(lambda g: (over_tiles(shifted(g), jnp.maximum),), (jnp.maximum,), rows)

        def leaf(g):
            s = shifted(g)
            e = jnp.exp(s - spread(peak, g, states))
            return (
                over_tiles(e, jnp.add),
                over_tiles(e * dirs[0], jnp.add),
                over_tiles(e * dirs[1], jnp.add),
                over_tiles(jnp.where(ids == spread(labels, g, states), s, 0.0), jnp.add),
            )

        total, mix0, mix1, anchor = fold(leaf, (jnp.add,) * 4, rows)
        inverse = 1.0 / total
        out_ref[0, pl.ds(at, ROWS), :] = peak + jnp.log(total)
        out_ref[1, pl.ds(at, ROWS), :] = mix0 * inverse
        out_ref[2, pl.ds(at, ROWS), :] = mix1 * inverse
        out_ref[3, pl.ds(at, ROWS), :] = anchor
        return carry

    lax.fori_loop(0, steps, step, 0)


def quarter_copy(flip, energies_hbm, quarter_ref, pieces):
    width = quarter_ref.shape[1]
    size = width // len(pieces)
    copies = []
    for i, sem in enumerate(pieces):
        source = energies_hbm.at[:, pl.ds(pl.multiple_of(spot(flip) * width + i * size, size), size)]
        copies.append(pltpu.make_async_copy(source, quarter_ref.at[:, pl.ds(i * size, size)], sem))
    return copies


def piecewise(flip, copies, out_ref, quarter_ref, labels_ref, base_ref, dirs_ref):
    width = quarter_ref.shape[1]
    n = max(len(copies), 1)
    size, rows = width // n, width // LANES // n
    for i in range(n):
        if copies:
            copies[i].wait()
        part = out_ref.at[:, pl.ds(i * rows, rows), :]
        row = spot(flip) * (width // LANES) + i * rows
        sums_of(part, quarter_ref, i * size, labels_ref, row, base_ref, dirs_ref, size // TILE)


def first_body(flips, pieces, counts_hbm, free_hbm, dirs_hbm, labels_hbm, energies_hbm, *refs):
    out_ref, base_ref, dirs_ref, labels_ref, *quarter_refs = refs[:-4]
    counts_s, free_s, dirs_s, sems = refs[-4:]
    states = base_ref.shape[0]
    own = quarter_copy(flips[0], energies_hbm, quarter_refs[0], [sems.at[i] for i in range(pieces)])
    small = [
        pltpu.make_async_copy(counts_hbm, counts_s, sems.at[pieces]),
        pltpu.make_async_copy(free_hbm, free_s, sems.at[pieces + 1]),
        pltpu.make_async_copy(dirs_hbm, dirs_s, sems.at[pieces + 2]),
    ]
    rows = labels_ref.shape[0] // 4
    marks = []
    for i in range(4):
        at = pl.ds(pl.multiple_of(jnp.bitwise_xor(spot(flips[0]), i) * rows, rows), rows)
        marks.append(pltpu.make_async_copy(labels_hbm.at[at, :], labels_ref.at[at, :], sems.at[pieces + 3 + i]))
    rest = []
    for k in range(1, len(flips)):
        rest += quarter_copy(flips[k], energies_hbm, quarter_refs[k], [sems.at[pieces + 6 + k]])
    for copy in small + own[:1] + marks[:1] + own[1:] + marks[1:] + rest:
        copy.start()
    for copy in small:
        copy.wait()
    base_ref[...] = bases(counts_s, free_s, states)
    dirs_ref[0] = column(dirs_s[0:1, :], states)
    dirs_ref[1] = column(dirs_s[1:2, :], states)
    marks[0].wait()
    piecewise(flips[0], own, out_ref, quarter_refs[0], labels_ref, base_ref, dirs_ref)
    for copy in marks[1:] + rest:
        copy.wait()


def later_body(flip, loads, pieces, base_ref, dirs_ref, labels_ref, *refs):
    own, rest = [], []
    if loads:
        energies_hbm, out_ref, *load_refs, sems = refs[-3 - len(loads) :]
        for k, (load, ref) in enumerate(zip(loads, load_refs, strict=True)):
            if load == flip:
                own = quarter_copy(load, energies_hbm, ref, [sems.at[len(loads) + i] for i in range(pieces)])
            else:
                rest += quarter_copy(load, energies_hbm, ref, [sems.at[k]])
        quarter_ref = load_refs[0] if own else refs[0]
    else:
        quarter_ref, out_ref = refs
    for copy in own + rest:
        copy.start()
    piecewise(flip, own, out_ref, quarter_ref, labels_ref, base_ref, dirs_ref)
    for copy in rest:
        copy.wait()


def tally_body(labels_ref, tally_ref):
    states = tally_ref.shape[0]
    first_state = lax.axis_index("state") * states
    ids = lax.broadcasted_iota(jnp.int32, (states, LANES), 0)

    def step(j, tally):
        labels = labels_ref[pl.ds(pl.multiple_of(j * ROWS, ROWS), ROWS), :] - first_state
        for g in range(ROWS):
            tally += jnp.where(ids == spread(labels, g, states), 1.0, 0.0)
        return tally

    tally_ref[...] = lax.fori_loop(0, labels_ref.shape[0] // ROWS, step, jnp.zeros((states, LANES), jnp.float32))


def weigh(part_ref, energies_ref, base_ref):
    states, size = energies_ref.shape

    def step(j, carry):
        occupancy, mix0, mix1 = carry
        at = pl.ds(pl.multiple_of(j * ROWS, ROWS), ROWS)
        norm, first, second = part_ref[0, at, :], part_ref[1, at, :], part_ref[2, at, :]
        for g in range(ROWS):
            cols = pl.ds(pl.multiple_of(j * TILE + g * LANES, LANES), LANES)
            w = jnp.exp((base_ref[...] - energies_ref[:, cols]) - spread(norm, g, states))
            occupancy += w
            mix0 += w * spread(first, g, states)
            mix1 += w * spread(second, g, states)
        return occupancy, mix0, mix1

    zero = jnp.zeros((states, LANES), jnp.float32)
    return lax.fori_loop(0, size // TILE, step, (zero, zero, zero))


def weigh_body(part_ref, base_ref, energies_ref, *refs):
    *before, sums_ref = refs
    for i, x in enumerate(weigh(part_ref, energies_ref, base_ref)):
        sums_ref[i] = x + before[0][i] if before else x


def last_body(part_ref, base_ref, energies_ref, dirs_ref, tally_ref, before_ref, out_ref):
    sums = [x + before_ref[i] for i, x in enumerate(weigh(part_ref, energies_ref, base_ref))]
    states = energies_ref.shape[0]
    eye = lax.broadcasted_iota(jnp.int32, (states, states), 0) == lax.broadcasted_iota(jnp.int32, (states, states), 1)

    def row(x):
        total = jnp.broadcast_to(jnp.sum(x, axis=1, keepdims=True), (states, states))
        return jnp.sum(jnp.where(eye, total, 0.0), axis=0, keepdims=True)

    out_ref[0:1, :] = row(sums[0] - tally_ref[...])
    for j in range(2):
        out_ref[j + 1 : j + 2, :] = row(dirs_ref[j] * sums[0] - sums[j + 1])


def place_body(flips, *refs):
    *part_refs, _, norm_hbm, anchor_hbm, sems = refs
    rows = part_refs[0].shape[1]
    copies = []
    for k, part_ref in enumerate(part_refs):
        at = pl.ds(pl.multiple_of(spot(flips[k]) * rows, rows), rows)
        copies.append(pltpu.make_async_copy(part_ref.at[0], norm_hbm.at[at, :], sems.at[2 * k]))
        copies.append(pltpu.make_async_copy(part_ref.at[3], anchor_hbm.at[at, :], sems.at[2 * k + 1]))
    for copy in copies:
        copy.start()
    for copy in copies:
        copy.wait()


def total_body(scale, mine_ref, other_ref, gradient_hbm, products_hbm, gradient_s, products_s, sems):
    total = scale * (mine_ref[...] + other_ref[...])
    gradient_s[...] = total[0:1]
    products_s[...] = total[1:3]
    copies = [
        pltpu.make_async_copy(gradient_s, gradient_hbm, sems.at[0]),
        pltpu.make_async_copy(products_s, products_hbm, sems.at[1]),
    ]
    for copy in copies:
        copy.start()
    for copy in copies:
        copy.wait()


def unite(parts, out_ref, last=False):
    norms = [part[0] for part in parts]
    peak = functools.reduce(jnp.maximum, norms)
    scales = [jnp.exp(norm - peak) for norm in norms]
    total = functools.reduce(jnp.add, scales)
    inverse = 1.0 / total
    norm = peak + jnp.log(total)
    anchor = functools.reduce(jnp.add, [part[3] for part in parts])
    out_ref[0] = norm
    for j in (1, 2):
        out_ref[j] = functools.reduce(jnp.add, [s * part[j] for s, part in zip(scales, parts, strict=True)]) * inverse
    out_ref[3] = anchor - norm if last else anchor


def merge_body(last, *refs):
    unite(refs[:-1], refs[-1], last)


VMEM = pl.BlockSpec(memory_space=pltpu.VMEM)
HBM = pl.BlockSpec(memory_space=pltpu.HBM)
LIMIT = 16 * 1024 * 1024


def f32(*shape):
    return jax.ShapeDtypeStruct(shape, jnp.float32)


def kernel(body, in_specs, out_specs, out_shape, name, work, scratch=()):
    return pl.pallas_call(
        body,
        in_specs=in_specs,
        out_specs=out_specs,
        out_shape=out_shape,
        scratch_shapes=list(scratch),
        compiler_params=pltpu.CompilerParams(vmem_limit_bytes=LIMIT),
        cost_estimate=pl.CostEstimate(flops=work // 1024, bytes_accessed=1024, transcendentals=0),
        name=name,
    )


def local(energies, counts, labels, free_energy, directions):
    states, samples = energies.shape
    width, cores = lax.axis_size("state"), lax.axis_size("sample")
    near, side, across, stay = 2, 1, 3, 0
    order, loads = (across, near, side, stay), LOADS
    rows = samples // 4 // LANES
    work = states * rows * LANES
    labels_in = labels.reshape(samples // LANES, LANES)
    part = f32(4, rows, LANES)
    pieces = 8 if rows % (8 * ROWS) == 0 else 1
    quarter = f32(states, samples // 4)
    energies = pltpu.with_memory_space_constraint(energies, pltpu.HBM)

    first, base, dirs, labels, *quarters = kernel(
        functools.partial(first_body, order[: loads[0]], pieces),
        [HBM] * 5,
        [VMEM] * (4 + loads[0]),
        [
            part,
            f32(states, LANES),
            f32(2, states, LANES),
            jax.ShapeDtypeStruct(labels_in.shape, labels_in.dtype),
        ]
        + [quarter] * loads[0],
        "first_sums",
        work,
        [
            pltpu.VMEM((1, states), jnp.int32),
            pltpu.VMEM((1, states), jnp.float32),
            pltpu.VMEM((2, states), jnp.float32),
            pltpu.SemaphoreType.DMA((pieces + 6 + loads[0],)),
        ],
    )(
        *(
            pltpu.with_memory_space_constraint(x, pltpu.HBM)
            for x in (counts.reshape(1, states), free_energy.reshape(1, states), directions, labels_in)
        ),
        energies,
    )

    def sums_for(k, name):
        have = len(quarters)
        more = order[have : have + (loads[k] if k < len(loads) else 0)]
        args = [base, dirs, labels] + ([quarters[k]] if k < have else []) + ([energies] if more else [])
        out, *loaded = kernel(
            functools.partial(later_body, order[k], more, pieces),
            [VMEM] * (len(args) - bool(more)) + [HBM] * bool(more),
            [VMEM] * (1 + len(more)),
            [part] + [quarter] * len(more),
            name,
            work,
            [pltpu.SemaphoreType.DMA((len(more) + pieces,))] if more else [],
        )(*args)
        quarters.extend(loaded)
        return out

    def send(x, flip):
        return lax.ppermute(x, "state", [(place, place ^ flip) for place in range(width)])

    def weigh_part(k, x, before, name):
        args = [x, base, quarters[k], *before]
        return kernel(weigh_body, [VMEM] * len(args), VMEM, f32(3, states, LANES), name, work)(*args)

    def merge(parts, last, name):
        return kernel(functools.partial(merge_body, last), [VMEM] * len(parts), VMEM, part, name, work)(*parts)

    far = range(2, int(math.log2(width)))
    got_side = send(first, near)
    got_near = send(sums_for(1, "near_sums"), near)
    pair = merge([sums_for(2, "side_sums"), got_side], False, "merge_pair")
    got_pair = send(pair, side)
    union = merge([sums_for(3, "own_sums"), got_near], False, "merge_near")
    union = merge([union, got_pair], not far, "merge_square")
    tally = kernel(tally_body, [VMEM], VMEM, f32(states, LANES), "tally", work)(labels)
    for bit in far:
        union = merge([union, send(union, 1 << bit)], bit == far[-1], "merge_far")
    ends = [(3, union)] + [(k, send(union, order[k])) for k in range(3)]
    sums = []
    for k, x in ends[:-1]:
        sums = [weigh_part(k, x, sums, f"weigh{k}")]
    k, x = ends[-1]
    mine = kernel(last_body, [VMEM] * 6, VMEM, f32(3, states), "last_sums", work)(
        x, base, quarters[k], dirs, tally, *sums
    )
    other = lax.ppermute(mine, "sample", [(c, cores - 1 - c) for c in range(cores)])
    long = f32(samples // LANES, LANES)
    log_norm, anchor_logp = kernel(
        functools.partial(place_body, tuple(order[k] for k, _ in ends)),
        [VMEM] * (len(ends) + 1),
        [HBM] * 2,
        [long, long],
        "place",
        1024,
        [pltpu.SemaphoreType.DMA((2 * len(ends),))],
    )(*(x for _, x in ends), mine)
    gradient, products = kernel(
        functools.partial(total_body, states * width / (samples * cores)),
        [VMEM] * 2,
        [HBM] * 2,
        [f32(1, states), f32(2, states)],
        "totals",
        1024,
        [pltpu.VMEM((1, states), jnp.float32), pltpu.VMEM((2, states), jnp.float32), pltpu.SemaphoreType.DMA((2,))],
    )(mine, other)
    return log_norm.reshape(samples), anchor_logp.reshape(samples), gradient.reshape(states), products


def solution(mesh):
    return jax.shard_map(
        local,
        mesh=mesh,
        in_specs=(
            P(("group", "state"), "sample"),
            P(("group", "state")),
            P(("group", "sample")),
            P(("group", "state")),
            P(None, ("group", "state")),
        ),
        out_specs=(
            P(("group", "sample")),
            P(("group", "sample")),
            P(("group", "state")),
            P(None, ("group", "state")),
        ),
        check_vma=False,
    )
```

```python
import functools
import math

import jax
import jax.numpy as jnp
from jax import lax
from jax.experimental import pallas as pl
from jax.experimental.pallas import tpu as pltpu
from jax.sharding import PartitionSpec as P

LANES = 128
ROWS = 8
TILE = LANES * ROWS
LOADS = (1, 3)
NEAR = (2, 2)
GATHER = ((3, 2), (2, 1), (1, 3))


def plan(level, shift):
    if level == 0:
        return [0] * ROWS, 1
    half = ROWS >> level
    first, count = plan(level - 1, shift)
    second, _ = plan(level - 1, shift - half)
    owner = []
    for row in range(ROWS):
        keep = ((row - shift) // half) % 2 == 1
        owner.append(first[row] if keep else second[row] + count)
    return owner, 2 * count


PLACE, _ = plan(3, 0)


def fold(leaf, combine, rows, level=3, shift=0, first=0):
    if level == 0:
        return leaf(PLACE.index(first))
    half = ROWS >> level
    count = 1 << (level - 1)
    a = fold(leaf, combine, rows, level - 1, shift, first)
    b = fold(leaf, combine, rows, level - 1, shift - half, first + count)
    keep = (((rows - shift + 2 * ROWS) // half) % 2) == 1
    out = []
    for one, two, how in zip(a, b, combine, strict=True):
        mine = jnp.where(keep, one, two)
        other = jnp.where(keep, two, one)
        out.append(how(mine, pltpu.roll(other, half, 0)))
    return tuple(out)


def column(row, states):
    spread = jnp.broadcast_to(row, (states, states))
    eye = lax.broadcasted_iota(jnp.int32, (states, states), 0) == lax.broadcasted_iota(jnp.int32, (states, states), 1)
    picked = jnp.sum(jnp.where(eye, spread, 0.0), axis=1, keepdims=True)
    return jnp.broadcast_to(picked, (states, LANES))


def bases(counts_ref, free_ref, states):
    return column(jnp.log(counts_ref[...].astype(jnp.float32)) + free_ref[...], states)


def odd_core():
    return lax.axis_index("sample") % 2 == 1


def spot(flips):
    flip = jnp.where(odd_core(), flips[1], flips[0]) if flips[0] != flips[1] else flips[0]
    return jnp.bitwise_xor(jnp.bitwise_and(lax.axis_index("state"), 3), flip)


def over_tiles(x, how):
    parts = [x[i * ROWS : (i + 1) * ROWS] for i in range(x.shape[0] // ROWS)]
    return functools.reduce(how, parts)


def spread(x, g, states):
    return jnp.broadcast_to(x[g : g + 1, :], (states, LANES))


def sums_of(out_ref, energies_ref, offset, labels_ref, label_row, base, dirs, steps):
    states = energies_ref.shape[0]
    rows = lax.broadcasted_iota(jnp.int32, (ROWS, LANES), 0)
    ids = lax.broadcasted_iota(jnp.int32, (states, LANES), 0)
    first_state = lax.axis_index("state") * states

    def step(j, carry):
        at = pl.multiple_of(j * ROWS, ROWS)
        labels = labels_ref[pl.ds(pl.multiple_of(label_row + j * ROWS, ROWS), ROWS), :] - first_state

        def shifted(g):
            cols = pl.ds(pl.multiple_of(offset + j * TILE + g * LANES, LANES), LANES)
            return base[...] - energies_ref[:, cols]

        (peak,) = fold(lambda g: (over_tiles(shifted(g), jnp.maximum),), (jnp.maximum,), rows)

        def leaf(g):
            s = shifted(g)
            e = jnp.exp(s - spread(peak, g, states))
            return (
                over_tiles(e, jnp.add),
                over_tiles(e * dirs[0], jnp.add),
                over_tiles(e * dirs[1], jnp.add),
                over_tiles(jnp.where(ids == spread(labels, g, states), s, 0.0), jnp.add),
            )

        total, mix0, mix1, anchor = fold(leaf, (jnp.add,) * 4, rows)
        inverse = 1.0 / total
        out_ref[0, pl.ds(at, ROWS), :] = peak + jnp.log(total)
        out_ref[1, pl.ds(at, ROWS), :] = mix0 * inverse
        out_ref[2, pl.ds(at, ROWS), :] = mix1 * inverse
        out_ref[3, pl.ds(at, ROWS), :] = anchor
        return carry

    lax.fori_loop(0, steps, step, 0)


def quarter_copy(flip, energies_hbm, quarter_ref, pieces):
    width = quarter_ref.shape[1]
    size = width // len(pieces)
    copies = []
    for i, sem in enumerate(pieces):
        source = energies_hbm.at[:, pl.ds(pl.multiple_of(spot(flip) * width + i * size, size), size)]
        copies.append(pltpu.make_async_copy(source, quarter_ref.at[:, pl.ds(i * size, size)], sem))
    return copies


def piecewise(flip, copies, out_ref, quarter_ref, labels_ref, base_ref, dirs_ref):
    width = quarter_ref.shape[1]
    n = max(len(copies), 1)
    size, rows = width // n, width // LANES // n
    for i in range(n):
        if copies:
            copies[i].wait()
        part = out_ref.at[:, pl.ds(i * rows, rows), :]
        row = spot(flip) * (width // LANES) + i * rows
        sums_of(part, quarter_ref, i * size, labels_ref, row, base_ref, dirs_ref, size // TILE)


def first_body(flips, pieces, counts_hbm, free_hbm, dirs_hbm, labels_hbm, energies_hbm, *refs):
    out_ref, base_ref, dirs_ref, labels_ref, *quarter_refs = refs[:-4]
    counts_s, free_s, dirs_s, sems = refs[-4:]
    states = base_ref.shape[0]
    own = quarter_copy(flips[0], energies_hbm, quarter_refs[0], [sems.at[i] for i in range(pieces)])
    small = [
        pltpu.make_async_copy(counts_hbm, counts_s, sems.at[pieces]),
        pltpu.make_async_copy(free_hbm, free_s, sems.at[pieces + 1]),
        pltpu.make_async_copy(dirs_hbm, dirs_s, sems.at[pieces + 2]),
    ]
    rows = labels_ref.shape[0] // 4
    marks = []
    for i in range(4):
        at = pl.ds(pl.multiple_of(jnp.bitwise_xor(spot(flips[0]), i) * rows, rows), rows)
        marks.append(pltpu.make_async_copy(labels_hbm.at[at, :], labels_ref.at[at, :], sems.at[pieces + 3 + i]))
    rest = []
    for k in range(1, len(flips)):
        rest += quarter_copy(flips[k], energies_hbm, quarter_refs[k], [sems.at[pieces + 6 + k]])
    for copy in small + own[:1] + marks[:1] + own[1:] + marks[1:] + rest:
        copy.start()
    for copy in small:
        copy.wait()
    base_ref[...] = bases(counts_s, free_s, states)
    dirs_ref[0] = column(dirs_s[0:1, :], states)
    dirs_ref[1] = column(dirs_s[1:2, :], states)
    marks[0].wait()
    piecewise(flips[0], own, out_ref, quarter_refs[0], labels_ref, base_ref, dirs_ref)
    for copy in marks[1:] + rest:
        copy.wait()


def later_body(flip, loads, pieces, base_ref, dirs_ref, labels_ref, *refs):
    own, rest = [], []
    if loads:
        energies_hbm, out_ref, *load_refs, sems = refs[-3 - len(loads) :]
        for k, (load, ref) in enumerate(zip(loads, load_refs, strict=True)):
            if load == flip:
                own = quarter_copy(load, energies_hbm, ref, [sems.at[len(loads) + i] for i in range(pieces)])
            else:
                rest += quarter_copy(load, energies_hbm, ref, [sems.at[k]])
        quarter_ref = load_refs[0] if own else refs[0]
    else:
        quarter_ref, out_ref = refs
    for copy in own + rest:
        copy.start()
    piecewise(flip, own, out_ref, quarter_ref, labels_ref, base_ref, dirs_ref)
    for copy in rest:
        copy.wait()


def tally_body(labels_ref, tally_ref):
    states = tally_ref.shape[0]
    first_state = lax.axis_index("state") * states
    ids = lax.broadcasted_iota(jnp.int32, (states, LANES), 0)

    def step(j, tally):
        labels = labels_ref[pl.ds(pl.multiple_of(j * ROWS, ROWS), ROWS), :] - first_state
        for g in range(ROWS):
            tally += jnp.where(ids == spread(labels, g, states), 1.0, 0.0)
        return tally

    tally_ref[...] = lax.fori_loop(0, labels_ref.shape[0] // ROWS, step, jnp.zeros((states, LANES), jnp.float32))


def weigh(part_ref, energies_ref, base_ref):
    states, size = energies_ref.shape

    def step(j, carry):
        occupancy, mix0, mix1 = carry
        at = pl.ds(pl.multiple_of(j * ROWS, ROWS), ROWS)
        norm, first, second = part_ref[0, at, :], part_ref[1, at, :], part_ref[2, at, :]
        for g in range(ROWS):
            cols = pl.ds(pl.multiple_of(j * TILE + g * LANES, LANES), LANES)
            w = jnp.exp((base_ref[...] - energies_ref[:, cols]) - spread(norm, g, states))
            occupancy += w
            mix0 += w * spread(first, g, states)
            mix1 += w * spread(second, g, states)
        return occupancy, mix0, mix1

    zero = jnp.zeros((states, LANES), jnp.float32)
    return lax.fori_loop(0, size // TILE, step, (zero, zero, zero), unroll=4)


def weigh_either(part_ref, base_ref, even_ref, odd_ref, sums_ref, before_ref=None):
    def weigh_in(energies_ref):
        for i, x in enumerate(weigh(part_ref, energies_ref, base_ref)):
            sums_ref[i] = x + before_ref[i] if before_ref is not None else x

    if even_ref is odd_ref:
        weigh_in(even_ref)
    else:
        pl.when(odd_core())(lambda: weigh_in(odd_ref))
        pl.when(jnp.logical_not(odd_core()))(lambda: weigh_in(even_ref))


def weigh_body(same, *refs):
    *refs, sums_ref = refs
    part_ref, base_ref, *refs = refs
    even_ref, odd_ref, *before = [refs[0], *refs] if same else refs
    weigh_either(part_ref, base_ref, even_ref, odd_ref, sums_ref, *before)


def last_body(part_ref, base_ref, even_ref, odd_ref, dirs_ref, tally_ref, before_ref, out_ref, sums_s):
    weigh_either(part_ref, base_ref, even_ref, odd_ref, sums_s, before_ref)
    sums = sums_s[0], sums_s[1], sums_s[2]
    states = even_ref.shape[0]
    eye = lax.broadcasted_iota(jnp.int32, (states, states), 0) == lax.broadcasted_iota(jnp.int32, (states, states), 1)

    def row(x):
        total = jnp.broadcast_to(jnp.sum(x, axis=1, keepdims=True), (states, states))
        return jnp.sum(jnp.where(eye, total, 0.0), axis=0, keepdims=True)

    out_ref[0:1, :] = row(sums[0] - tally_ref[...])
    for j in range(2):
        out_ref[j + 1 : j + 2, :] = row(dirs_ref[j] * sums[0] - sums[j + 1])


def place_body(flips, *refs):
    *part_refs, _, norm_hbm, anchor_hbm, sems = refs
    rows = part_refs[0].shape[1]
    copies = []
    for k, part_ref in enumerate(part_refs):
        at = pl.ds(pl.multiple_of(spot(flips[k]) * rows, rows), rows)
        copies.append(pltpu.make_async_copy(part_ref.at[0], norm_hbm.at[at, :], sems.at[2 * k]))
        copies.append(pltpu.make_async_copy(part_ref.at[3], anchor_hbm.at[at, :], sems.at[2 * k + 1]))
    for copy in copies:
        copy.start()
    for copy in copies:
        copy.wait()


def total_body(scale, mine_ref, other_ref, gradient_hbm, products_hbm, gradient_s, products_s, sems):
    total = scale * (mine_ref[...] + other_ref[...])
    gradient_s[...] = total[0:1]
    products_s[...] = total[1:3]
    copies = [
        pltpu.make_async_copy(gradient_s, gradient_hbm, sems.at[0]),
        pltpu.make_async_copy(products_s, products_hbm, sems.at[1]),
    ]
    for copy in copies:
        copy.start()
    for copy in copies:
        copy.wait()


def unite(parts, out_ref, last=False):
    norms = [part[0] for part in parts]
    peak = functools.reduce(jnp.maximum, norms)
    scales = [jnp.exp(norm - peak) for norm in norms]
    total = functools.reduce(jnp.add, scales)
    inverse = 1.0 / total
    norm = peak + jnp.log(total)
    anchor = functools.reduce(jnp.add, [part[3] for part in parts])
    out_ref[0] = norm
    for j in (1, 2):
        out_ref[j] = functools.reduce(jnp.add, [s * part[j] for s, part in zip(scales, parts, strict=True)]) * inverse
    out_ref[3] = anchor - norm if last else anchor


def merge_body(last, *refs):
    unite(refs[:-1], refs[-1], last)


VMEM = pl.BlockSpec(memory_space=pltpu.VMEM)
HBM = pl.BlockSpec(memory_space=pltpu.HBM)
LIMIT = 16 * 1024 * 1024


def f32(*shape):
    return jax.ShapeDtypeStruct(shape, jnp.float32)


def kernel(body, in_specs, out_specs, out_shape, name, work, scratch=()):
    return pl.pallas_call(
        body,
        in_specs=in_specs,
        out_specs=out_specs,
        out_shape=out_shape,
        scratch_shapes=list(scratch),
        compiler_params=pltpu.CompilerParams(vmem_limit_bytes=LIMIT),
        cost_estimate=pl.CostEstimate(flops=work // 1024, bytes_accessed=1024, transcendentals=0),
        name=name,
    )


def local(energies, counts, labels, free_energy, directions):
    states, samples = energies.shape
    width, cores = lax.axis_size("state"), lax.axis_size("sample")
    near, side, across, stay = NEAR, (3 - NEAR[0], 3 - NEAR[1]), (3, 3), (0, 0)
    order, loads = (across, near, side, stay), LOADS
    rows = samples // 4 // LANES
    work = states * rows * LANES
    labels_in = labels.reshape(samples // LANES, LANES)
    part = f32(4, rows, LANES)
    pieces = 8 if rows % (8 * ROWS) == 0 else 1
    quarter = f32(states, samples // 4)
    energies = pltpu.with_memory_space_constraint(energies, pltpu.HBM)

    first, base, dirs, labels, *quarters = kernel(
        functools.partial(first_body, order[: loads[0]], pieces),
        [HBM] * 5,
        [VMEM] * (4 + loads[0]),
        [
            part,
            f32(states, LANES),
            f32(2, states, LANES),
            jax.ShapeDtypeStruct(labels_in.shape, labels_in.dtype),
        ]
        + [quarter] * loads[0],
        "first_sums",
        work,
        [
            pltpu.VMEM((1, states), jnp.int32),
            pltpu.VMEM((1, states), jnp.float32),
            pltpu.VMEM((2, states), jnp.float32),
            pltpu.SemaphoreType.DMA((pieces + 6 + loads[0],)),
        ],
    )(
        *(
            pltpu.with_memory_space_constraint(x, pltpu.HBM)
            for x in (counts.reshape(1, states), free_energy.reshape(1, states), directions, labels_in)
        ),
        energies,
    )

    def sums_for(k, name):
        have = len(quarters)
        more = order[have : have + (loads[k] if k < len(loads) else 0)]
        args = [base, dirs, labels] + ([quarters[k]] if k < have else []) + ([energies] if more else [])
        out, *loaded = kernel(
            functools.partial(later_body, order[k], more, pieces),
            [VMEM] * (len(args) - bool(more)) + [HBM] * bool(more),
            [VMEM] * (1 + len(more)),
            [part] + [quarter] * len(more),
            name,
            work,
            [pltpu.SemaphoreType.DMA((len(more) + pieces,))] if more else [],
        )(*args)
        quarters.extend(loaded)
        return out

    def merge(parts, last, name):
        return kernel(functools.partial(merge_body, last), [VMEM] * len(parts), VMEM, part, name, work)(*parts)

    def send(x, flips):
        pairs = [(p * cores + c, (p ^ flips[c % 2]) * cores + c) for p in range(width) for c in range(cores)]
        return lax.ppermute(x, ("state", "sample"), pairs)

    def quarters_of(flips):
        picked = [quarters[[f[c] for f in order].index(flips[c])] for c in range(2)]
        return picked[:1] if picked[0] is picked[1] else picked

    def weigh_part(flips, x, before, name):
        energies = quarters_of(flips)
        args = [x, base, *energies, *before]
        body = functools.partial(weigh_body, len(energies) == 1)
        return kernel(body, [VMEM] * len(args), VMEM, f32(3, states, LANES), name, work)(*args)

    far = range(2, int(math.log2(width)))
    got_side = send(first, near)
    got_near = send(sums_for(1, "near_sums"), near)
    pair = merge([sums_for(2, "side_sums"), got_side], False, "merge_pair")
    got_pair = send(pair, side)
    union = merge([sums_for(3, "own_sums"), got_near], False, "merge_near")
    union = merge([union, got_pair], not far, "merge_square")
    tally = kernel(tally_body, [VMEM], VMEM, f32(states, LANES), "tally", work)(labels)
    for bit in far:
        union = merge([union, send(union, (1 << bit,) * 2)], bit == far[-1], "merge_far")
    ends = [(stay, union)] + [(flips, send(union, flips)) for flips in GATHER]
    sums = []
    for k, (flips, x) in enumerate(ends[:-1]):
        sums = [weigh_part(flips, x, sums, f"weigh{k}")]
    flips, x = ends[-1]
    last = quarters_of(flips)
    mine = kernel(
        last_body,
        [VMEM] * 7,
        VMEM,
        f32(3, states),
        "last_sums",
        work,
        [pltpu.VMEM((3, states, LANES), jnp.float32)],
    )(x, base, last[0], last[-1], dirs, tally, *sums)
    other = lax.ppermute(mine, "sample", [(c, cores - 1 - c) for c in range(cores)])
    long = f32(samples // LANES, LANES)
    log_norm, anchor_logp = kernel(
        functools.partial(place_body, tuple(flips for flips, _ in ends)),
        [VMEM] * (len(ends) + 1),
        [HBM] * 2,
        [long, long],
        "place",
        1024,
        [pltpu.SemaphoreType.DMA((2 * len(ends),))],
    )(*(x for _, x in ends), mine)
    gradient, products = kernel(
        functools.partial(total_body, states * width / (samples * cores)),
        [VMEM] * 2,
        [HBM] * 2,
        [f32(1, states), f32(2, states)],
        "totals",
        1024,
        [pltpu.VMEM((1, states), jnp.float32), pltpu.VMEM((2, states), jnp.float32), pltpu.SemaphoreType.DMA((2,))],
    )(mine, other)
    return log_norm.reshape(samples), anchor_logp.reshape(samples), gradient.reshape(states), products


def solution(mesh):
    return jax.shard_map(
        local,
        mesh=mesh,
        in_specs=(
            P(("group", "state"), "sample"),
            P(("group", "state")),
            P(("group", "sample")),
            P(("group", "state")),
            P(None, ("group", "state")),
        ),
        out_specs=(
            P(("group", "sample")),
            P(("group", "sample")),
            P(("group", "state")),
            P(None, ("group", "state")),
        ),
        check_vma=False,
    )
```

```python
import functools
import math

import jax
import jax.numpy as jnp
from jax import lax
from jax.experimental import pallas as pl
from jax.experimental.pallas import tpu as pltpu
from jax.sharding import PartitionSpec as P

LANES = 128
ROWS = 8
TILE = LANES * ROWS
LOADS = (1, 3)


def plan(level, shift):
    if level == 0:
        return [0] * ROWS, 1
    half = ROWS >> level
    first, count = plan(level - 1, shift)
    second, _ = plan(level - 1, shift - half)
    owner = []
    for row in range(ROWS):
        keep = ((row - shift) // half) % 2 == 1
        owner.append(first[row] if keep else second[row] + count)
    return owner, 2 * count


PLACE, _ = plan(3, 0)


def fold(leaf, combine, rows, level=3, shift=0, first=0):
    if level == 0:
        return leaf(PLACE.index(first))
    half = ROWS >> level
    count = 1 << (level - 1)
    a = fold(leaf, combine, rows, level - 1, shift, first)
    b = fold(leaf, combine, rows, level - 1, shift - half, first + count)
    keep = (((rows - shift + 2 * ROWS) // half) % 2) == 1
    out = []
    for one, two, how in zip(a, b, combine, strict=True):
        mine = jnp.where(keep, one, two)
        other = jnp.where(keep, two, one)
        out.append(how(mine, pltpu.roll(other, half, 0)))
    return tuple(out)


def column(row, states):
    spread = jnp.broadcast_to(row, (states, states))
    eye = lax.broadcasted_iota(jnp.int32, (states, states), 0) == lax.broadcasted_iota(jnp.int32, (states, states), 1)
    picked = jnp.sum(jnp.where(eye, spread, 0.0), axis=1, keepdims=True)
    return jnp.broadcast_to(picked, (states, LANES))


def bases(counts_ref, free_ref, states):
    return column(jnp.log(counts_ref[...].astype(jnp.float32)) + free_ref[...], states)


def spot(flip):
    return jnp.bitwise_xor(jnp.bitwise_and(lax.axis_index("state"), 3), flip)


def over_tiles(x, how):
    parts = [x[i * ROWS : (i + 1) * ROWS] for i in range(x.shape[0] // ROWS)]
    return functools.reduce(how, parts)


def spread(x, g, states):
    return jnp.broadcast_to(x[g : g + 1, :], (states, LANES))


def sums_of(out_ref, energies_ref, offset, labels_ref, label_row, base, dirs, steps):
    states = energies_ref.shape[0]
    rows = lax.broadcasted_iota(jnp.int32, (ROWS, LANES), 0)
    ids = lax.broadcasted_iota(jnp.int32, (states, LANES), 0)
    first_state = lax.axis_index("state") * states

    def step(j, carry):
        at = pl.multiple_of(j * ROWS, ROWS)
        labels = labels_ref[pl.ds(pl.multiple_of(label_row + j * ROWS, ROWS), ROWS), :] - first_state

        def shifted(g):
            cols = pl.ds(pl.multiple_of(offset + j * TILE + g * LANES, LANES), LANES)
            return base[...] - energies_ref[:, cols]

        (peak,) = fold(lambda g: (over_tiles(shifted(g), jnp.maximum),), (jnp.maximum,), rows)

        def leaf(g):
            s = shifted(g)
            e = jnp.exp(s - spread(peak, g, states))
            return (
                over_tiles(e, jnp.add),
                over_tiles(e * dirs[0], jnp.add),
                over_tiles(e * dirs[1], jnp.add),
                over_tiles(jnp.where(ids == spread(labels, g, states), s, 0.0), jnp.add),
            )

        total, mix0, mix1, anchor = fold(leaf, (jnp.add,) * 4, rows)
        inverse = 1.0 / total
        out_ref[0, pl.ds(at, ROWS), :] = peak + jnp.log(total)
        out_ref[1, pl.ds(at, ROWS), :] = mix0 * inverse
        out_ref[2, pl.ds(at, ROWS), :] = mix1 * inverse
        out_ref[3, pl.ds(at, ROWS), :] = anchor
        return carry

    lax.fori_loop(0, steps, step, 0)


def quarter_copy(flip, energies_hbm, quarter_ref, pieces):
    width = quarter_ref.shape[1]
    size = width // len(pieces)
    copies = []
    for i, sem in enumerate(pieces):
        source = energies_hbm.at[:, pl.ds(pl.multiple_of(spot(flip) * width + i * size, size), size)]
        copies.append(pltpu.make_async_copy(source, quarter_ref.at[:, pl.ds(i * size, size)], sem))
    return copies


def piecewise(flip, copies, out_ref, quarter_ref, labels_ref, base_ref, dirs_ref):
    width = quarter_ref.shape[1]
    n = max(len(copies), 1)
    size, rows = width // n, width // LANES // n
    for i in range(n):
        if copies:
            copies[i].wait()
        part = out_ref.at[:, pl.ds(i * rows, rows), :]
        row = spot(flip) * (width // LANES) + i * rows
        sums_of(part, quarter_ref, i * size, labels_ref, row, base_ref, dirs_ref, size // TILE)


def first_body(flips, pieces, counts_hbm, free_hbm, dirs_hbm, labels_hbm, energies_hbm, *refs):
    out_ref, base_ref, dirs_ref, labels_ref, *quarter_refs = refs[:-4]
    counts_s, free_s, dirs_s, sems = refs[-4:]
    states = base_ref.shape[0]
    own = quarter_copy(flips[0], energies_hbm, quarter_refs[0], [sems.at[i] for i in range(pieces)])
    small = [
        pltpu.make_async_copy(counts_hbm, counts_s, sems.at[pieces]),
        pltpu.make_async_copy(free_hbm, free_s, sems.at[pieces + 1]),
        pltpu.make_async_copy(dirs_hbm, dirs_s, sems.at[pieces + 2]),
    ]
    rows = labels_ref.shape[0] // 4
    marks = []
    for i in range(4):
        at = pl.ds(pl.multiple_of(jnp.bitwise_xor(spot(flips[0]), i) * rows, rows), rows)
        marks.append(pltpu.make_async_copy(labels_hbm.at[at, :], labels_ref.at[at, :], sems.at[pieces + 3 + i]))
    rest = []
    for k in range(1, len(flips)):
        rest += quarter_copy(flips[k], energies_hbm, quarter_refs[k], [sems.at[pieces + 6 + k]])
    for copy in small + own[:1] + marks[:1] + own[1:] + marks[1:] + rest:
        copy.start()
    for copy in small:
        copy.wait()
    base_ref[...] = bases(counts_s, free_s, states)
    dirs_ref[0] = column(dirs_s[0:1, :], states)
    dirs_ref[1] = column(dirs_s[1:2, :], states)
    marks[0].wait()
    piecewise(flips[0], own, out_ref, quarter_refs[0], labels_ref, base_ref, dirs_ref)
    for copy in marks[1:] + rest:
        copy.wait()


def later_body(flip, loads, pieces, base_ref, dirs_ref, labels_ref, *refs):
    own, rest = [], []
    if loads:
        energies_hbm, out_ref, *load_refs, sems = refs[-3 - len(loads) :]
        for k, (load, ref) in enumerate(zip(loads, load_refs, strict=True)):
            if load == flip:
                own = quarter_copy(load, energies_hbm, ref, [sems.at[len(loads) + i] for i in range(pieces)])
            else:
                rest += quarter_copy(load, energies_hbm, ref, [sems.at[k]])
        quarter_ref = load_refs[0] if own else refs[0]
    else:
        quarter_ref, out_ref = refs
    for copy in own + rest:
        copy.start()
    piecewise(flip, own, out_ref, quarter_ref, labels_ref, base_ref, dirs_ref)
    for copy in rest:
        copy.wait()


def tally_body(labels_ref, tally_ref):
    states = tally_ref.shape[0]
    first_state = lax.axis_index("state") * states
    ids = lax.broadcasted_iota(jnp.int32, (states, LANES), 0)

    def step(j, tally):
        labels = labels_ref[pl.ds(pl.multiple_of(j * ROWS, ROWS), ROWS), :] - first_state
        for g in range(ROWS):
            tally += jnp.where(ids == spread(labels, g, states), 1.0, 0.0)
        return tally

    tally_ref[...] = lax.fori_loop(0, labels_ref.shape[0] // ROWS, step, jnp.zeros((states, LANES), jnp.float32))


def weigh(part_ref, energies_ref, base_ref):
    states, size = energies_ref.shape

    def step(j, carry):
        occupancy, mix0, mix1 = carry
        at = pl.ds(pl.multiple_of(j * ROWS, ROWS), ROWS)
        norm, first, second = part_ref[0, at, :], part_ref[1, at, :], part_ref[2, at, :]
        for g in range(ROWS):
            cols = pl.ds(pl.multiple_of(j * TILE + g * LANES, LANES), LANES)
            w = jnp.exp((base_ref[...] - energies_ref[:, cols]) - spread(norm, g, states))
            occupancy += w
            mix0 += w * spread(first, g, states)
            mix1 += w * spread(second, g, states)
        return occupancy, mix0, mix1

    zero = jnp.zeros((states, LANES), jnp.float32)
    return lax.fori_loop(0, size // TILE, step, (zero, zero, zero))


def weigh_body(part_ref, base_ref, energies_ref, *refs):
    *before, sums_ref = refs
    for i, x in enumerate(weigh(part_ref, energies_ref, base_ref)):
        sums_ref[i] = x + before[0][i] if before else x


def last_body(part_ref, base_ref, energies_ref, dirs_ref, tally_ref, before_ref, out_ref):
    sums = [x + before_ref[i] for i, x in enumerate(weigh(part_ref, energies_ref, base_ref))]
    states = energies_ref.shape[0]
    eye = lax.broadcasted_iota(jnp.int32, (states, states), 0) == lax.broadcasted_iota(jnp.int32, (states, states), 1)

    def row(x):
        total = jnp.broadcast_to(jnp.sum(x, axis=1, keepdims=True), (states, states))
        return jnp.sum(jnp.where(eye, total, 0.0), axis=0, keepdims=True)

    out_ref[0:1, :] = row(sums[0] - tally_ref[...])
    for j in range(2):
        out_ref[j + 1 : j + 2, :] = row(dirs_ref[j] * sums[0] - sums[j + 1])


def place_body(flips, *refs):
    *part_refs, _, norm_hbm, anchor_hbm, sems = refs
    rows = part_refs[0].shape[1]
    copies = []
    for k, part_ref in enumerate(part_refs):
        at = pl.ds(pl.multiple_of(spot(flips[k]) * rows, rows), rows)
        copies.append(pltpu.make_async_copy(part_ref.at[0], norm_hbm.at[at, :], sems.at[2 * k]))
        copies.append(pltpu.make_async_copy(part_ref.at[3], anchor_hbm.at[at, :], sems.at[2 * k + 1]))
    for copy in copies:
        copy.start()
    for copy in copies:
        copy.wait()


def total_body(scale, mine_ref, other_ref, gradient_hbm, products_hbm, gradient_s, products_s, sems):
    total = scale * (mine_ref[...] + other_ref[...])
    gradient_s[...] = total[0:1]
    products_s[...] = total[1:3]
    copies = [
        pltpu.make_async_copy(gradient_s, gradient_hbm, sems.at[0]),
        pltpu.make_async_copy(products_s, products_hbm, sems.at[1]),
    ]
    for copy in copies:
        copy.start()
    for copy in copies:
        copy.wait()


def unite(parts, out_ref, last=False):
    norms = [part[0] for part in parts]
    peak = functools.reduce(jnp.maximum, norms)
    scales = [jnp.exp(norm - peak) for norm in norms]
    total = functools.reduce(jnp.add, scales)
    inverse = 1.0 / total
    norm = peak + jnp.log(total)
    anchor = functools.reduce(jnp.add, [part[3] for part in parts])
    out_ref[0] = norm
    for j in (1, 2):
        out_ref[j] = functools.reduce(jnp.add, [s * part[j] for s, part in zip(scales, parts, strict=True)]) * inverse
    out_ref[3] = anchor - norm if last else anchor


def merge_body(last, *refs):
    unite(refs[:-1], refs[-1], last)


VMEM = pl.BlockSpec(memory_space=pltpu.VMEM)
HBM = pl.BlockSpec(memory_space=pltpu.HBM)
LIMIT = 16 * 1024 * 1024


def f32(*shape):
    return jax.ShapeDtypeStruct(shape, jnp.float32)


def kernel(body, in_specs, out_specs, out_shape, name, work, scratch=()):
    return pl.pallas_call(
        body,
        in_specs=in_specs,
        out_specs=out_specs,
        out_shape=out_shape,
        scratch_shapes=list(scratch),
        compiler_params=pltpu.CompilerParams(vmem_limit_bytes=LIMIT),
        cost_estimate=pl.CostEstimate(flops=work // 1024, bytes_accessed=1024, transcendentals=0),
        name=name,
    )


def local(energies, counts, labels, free_energy, directions):
    states, samples = energies.shape
    width, cores = lax.axis_size("state"), lax.axis_size("sample")
    near, side, across, stay = 2, 1, 3, 0
    order, loads = (across, near, stay, side), LOADS
    rows = samples // 4 // LANES
    work = states * rows * LANES
    labels_in = labels.reshape(samples // LANES, LANES)
    part = f32(4, rows, LANES)
    pieces = 8 if rows % (8 * ROWS) == 0 else 1
    quarter = f32(states, samples // 4)
    energies = pltpu.with_memory_space_constraint(energies, pltpu.HBM)

    first, base, dirs, labels, *quarters = kernel(
        functools.partial(first_body, order[: loads[0]], pieces),
        [HBM] * 5,
        [VMEM] * (4 + loads[0]),
        [
            part,
            f32(states, LANES),
            f32(2, states, LANES),
            jax.ShapeDtypeStruct(labels_in.shape, labels_in.dtype),
        ]
        + [quarter] * loads[0],
        "first_sums",
        work,
        [
            pltpu.VMEM((1, states), jnp.int32),
            pltpu.VMEM((1, states), jnp.float32),
            pltpu.VMEM((2, states), jnp.float32),
            pltpu.SemaphoreType.DMA((pieces + 6 + loads[0],)),
        ],
    )(
        *(
            pltpu.with_memory_space_constraint(x, pltpu.HBM)
            for x in (counts.reshape(1, states), free_energy.reshape(1, states), directions, labels_in)
        ),
        energies,
    )

    def sums_for(k, name):
        have = len(quarters)
        more = order[have : have + (loads[k] if k < len(loads) else 0)]
        args = [base, dirs, labels] + ([quarters[k]] if k < have else []) + ([energies] if more else [])
        out, *loaded = kernel(
            functools.partial(later_body, order[k], more, pieces),
            [VMEM] * (len(args) - bool(more)) + [HBM] * bool(more),
            [VMEM] * (1 + len(more)),
            [part] + [quarter] * len(more),
            name,
            work,
            [pltpu.SemaphoreType.DMA((len(more) + pieces,))] if more else [],
        )(*args)
        quarters.extend(loaded)
        return out

    def send(x, flip):
        return lax.ppermute(x, "state", [(place, place ^ flip) for place in range(width)])

    def weigh_part(k, x, before, name):
        args = [x, base, quarters[k], *before]
        return kernel(weigh_body, [VMEM] * len(args), VMEM, f32(3, states, LANES), name, work)(*args)

    def merge(parts, last, name):
        return kernel(functools.partial(merge_body, last), [VMEM] * len(parts), VMEM, part, name, work)(*parts)

    far = range(2, int(math.log2(width)))
    got_side = send(first, near)
    got_near = send(sums_for(1, "near_sums"), near)
    pair = merge([sums_for(3, "side_sums"), got_side], False, "merge_pair")
    got_pair = send(pair, side)
    union = merge([sums_for(2, "own_sums"), got_near], False, "merge_near")
    union = merge([union, got_pair], not far, "merge_square")
    tally = kernel(tally_body, [VMEM], VMEM, f32(states, LANES), "tally", work)(labels)
    for bit in far:
        union = merge([union, send(union, 1 << bit)], bit == far[-1], "merge_far")
    ends = [(2, union)] + [(k, send(union, order[k])) for k in (0, 1, 3)]
    sums = []
    for k, x in ends[:-1]:
        sums = [weigh_part(k, x, sums, f"weigh{k}")]
    k, x = ends[-1]
    mine = kernel(last_body, [VMEM] * 6, VMEM, f32(3, states), "last_sums", work)(
        x, base, quarters[k], dirs, tally, *sums
    )
    other = lax.ppermute(mine, "sample", [(c, cores - 1 - c) for c in range(cores)])
    long = f32(samples // LANES, LANES)
    log_norm, anchor_logp = kernel(
        functools.partial(place_body, tuple(order[k] for k, _ in ends)),
        [VMEM] * (len(ends) + 1),
        [HBM] * 2,
        [long, long],
        "place",
        1024,
        [pltpu.SemaphoreType.DMA((2 * len(ends),))],
    )(*(x for _, x in ends), mine)
    gradient, products = kernel(
        functools.partial(total_body, states * width / (samples * cores)),
        [VMEM] * 2,
        [HBM] * 2,
        [f32(1, states), f32(2, states)],
        "totals",
        1024,
        [pltpu.VMEM((1, states), jnp.float32), pltpu.VMEM((2, states), jnp.float32), pltpu.SemaphoreType.DMA((2,))],
    )(mine, other)
    return log_norm.reshape(samples), anchor_logp.reshape(samples), gradient.reshape(states), products


def solution(mesh):
    return jax.shard_map(
        local,
        mesh=mesh,
        in_specs=(
            P(("group", "state"), "sample"),
            P(("group", "state")),
            P(("group", "sample")),
            P(("group", "state")),
            P(None, ("group", "state")),
        ),
        out_specs=(
            P(("group", "sample")),
            P(("group", "sample")),
            P(("group", "state")),
            P(None, ("group", "state")),
        ),
        check_vma=False,
    )
```
